128 devices in a mesh: sec: 4 (over z_lo, core), gx: 8 (over x, z_hi), gy: 4 (over y).
Axes of the slice: x: 4, y: 4, z: 4 (z_hi: 2, z_lo: 2; z = z_hi * 2 + z_lo), core: 2. Of those that a mesh axis runs over, the one named last changes fastest.
Arguments:
- surface: float32 [64, 2, 256, 512], P(None, None, 'gx', 'gy'), may hold values from -6 to 6
- coef_table: float32 [64, 9, 2, 64], replicated, may hold values from -0.3 to 0.3
- vel_index: int32 [4, 256, 512], P('sec', 'gx', 'gy'), may hold values from 0 to 63
Outputs:
- image: float32 [4, 256, 512], P('sec', 'gx', 'gy')
The draws below stay inside these ranges and needn't reach their ends.
All inputs are finite; a program needn't handle non-finite values.
Results may differ from the reference program's by a relative error of at most 0.0003.
Values sent between devices are 32-bit elements; how exact they have to be, the bound alone decides.
No kernel may reach another device: no remote copies, remote signals or barrier semaphores. Data moves between devices by JAX's collectives and lax.ppermute only.
A program may use at most 128 MiB of HBM per device.

```python
import jax
import jax.numpy as jnp
from jax import lax

NF = 64
KT = 8
NV = 64
NX = 256
NY = 512
DEPTHS = 4


def touch_ends(drawn, key, least, top_value):
    extent = drawn.shape
    index_at = [jax.random.randint(jax.random.fold_in(key, axis), (), 0, extent[axis]) for axis in range(len(extent))]
    drawn = drawn.at[tuple(index_at)].set(least)
    longest = extent.index(max(extent))
    index_at[longest] = (index_at[longest] + 1) % extent[longest]
    return drawn.at[tuple(index_at)].set(top_value)


def block_levels(key, shape, split, low, top_value):
    factor_of, own = 1.0, jax.random.fold_in(key, 6)
    for dim, blocks in split:
        steps = jnp.exp(jax.random.uniform(jax.random.fold_in(own, dim), (blocks,), jnp.float32, low / len(split), top_value / len(split)))
        factor_of = factor_of * jnp.repeat(steps, shape[dim] // blocks).reshape([-1 if axis == dim else 1 for axis in range(len(shape))])
    return factor_of


def scatter_about(key, extent, spread, most, cuts=(), dtype=jnp.bfloat16):
    values = jax.random.normal(key, extent, jnp.float32) * spread
    if len(cuts) > 0:
        values = block_levels(key, extent, cuts, -0.22, 0.18) * values
    return jnp.clip(values, min=-most, max=most).astype(dtype)


def setup_inputs(seed: int = 0) -> dict:
    key_list = jax.random.split(jax.random.key(seed), 4)
    surface = scatter_about(key_list[0], (NF, 2, NX, NY), 1.0, 6.0, ((2, 8), (3, 4)), jnp.float32)
    coef_table = jnp.clip(jax.random.uniform(key_list[1], (NF, KT + 1, 2, NV), jnp.float32, -0.3, 0.3), -0.3, 0.3)
    vel_index = touch_ends(jax.random.randint(key_list[2], (DEPTHS, NX, NY), 0, NV), jax.random.fold_in(key_list[2], 1), 0, NV - 1).astype(jnp.int32)
    return dict(surface=surface, coef_table=coef_table, vel_index=vel_index)


def mclellan(field):
    padded = jnp.pad(field, ((0, 0), (1, 1), (1, 1)))
    rows = padded[:, :-2, :] + 2.0 * padded[:, 1:-1, :] + padded[:, 2:, :]
    both = rows[:, :, :-2] + 2.0 * rows[:, :, 1:-1] + rows[:, :, 2:]
    return 0.125 * both - field


def complex_mul(coeff, field):
    real = coeff[0] * field[0] - coeff[1] * field[1]
    imag = coeff[0] * field[1] + coeff[1] * field[0]
    return jnp.stack([real, imag])


def one_frequency(inputs):
    field, table, index = inputs
    images = []
    for depth in range(DEPTHS):
        coeffs = table[:, :, index[depth]]
        before = field
        current = mclellan(field)
        total = complex_mul(coeffs[0], before) + complex_mul(coeffs[1], current)
        for order in range(2, KT + 1):
            nxt = 2.0 * mclellan(current) - before
            total = total + complex_mul(coeffs[order], nxt)
            before, current = current, nxt
        field = total
        images.append(field[0])
    return jnp.stack(images)


def reference(surface, coef_table, vel_index):
    per_freq = lax.map(lambda pair: one_frequency((pair[0], pair[1], vel_index)), (surface, coef_table))
    return jnp.sum(per_freq, axis=0)
```

```python
import jax
import jax.numpy as jnp
from jax import lax
from jax.experimental import pallas as pl
from jax.experimental.pallas import tpu as pltpu
from jax.sharding import PartitionSpec as P

AXES = ("sec", "gx", "gy")
ROWS = 160
BLK = 20
TOP = 8
DEPTHS = 4
NV = 64


def flat(x, y, zh, zl, core):
    return ((zl * 2 + core) * 8 + x * 2 + zh) * 4 + y


def half_x(half, xq):
    return xq if half == 0 else 3 - xq


def groups_of_half():
    return [
        [
            flat(half_x(half, xq), y, zh, zl, core)
            for xq in range(2)
            for zh in range(2)
            for zl in range(2)
            for y in range(4)
        ]
        for half in range(2)
        for core in range(2)
    ]


def all_devices():
    for x in range(4):
        for y in range(4):
            for zh in range(2):
                for zl in range(2):
                    for core in range(2):
                        yield x, y, zh, zl, core


def core_pairs():
    return [(flat(*d), flat(*d[:4], 1 - d[4])) for d in all_devices()]


def half_pairs():
    return [(flat(*d), flat(3 - d[0], *d[1:])) for d in all_devices()]


def kernel(place, recv, halo, vel_other, halo_vel_other, table, out, nat, natv, term, img):
    half = place[0]
    core = place[1]
    lane = lax.broadcasted_iota(jnp.int32, (8, 128), 1)
    sub = lax.broadcasted_iota(jnp.int32, (8, 128), 0)
    quarter = lane // 32
    first = lane == 0
    last = lane == 127

    def interleave(chunks):
        res = []
        for v in range(4):
            idx = (lane % 32) * 4 + v
            got = [jnp.take_along_axis(c, idx, axis=1, mode="promise_in_bounds") for c in chunks]
            res.append(
                jnp.where(
                    quarter < 2,
                    jnp.where(quarter == 0, got[0], got[1]),
                    jnp.where(quarter == 2, got[2], got[3]),
                )
            )
        return res

    def place_rows(load, dst, lead, row0, convert):
        for rg in range(4):
            vs = interleave([load(y, rg) for y in range(4)])
            for v in range(4):
                val = vs[v].astype(jnp.int32) if convert else vs[v]
                dst[lead, v, pl.ds(pl.multiple_of(row0 + rg * 8, 8), 8), :] = val

    def tile_row(xq, zh):
        return jnp.where(half == 0, 2 * xq + zh, 3 - 2 * xq + zh) * 32

    @pl.loop(0, 8)
    def _(n):
        xq, zh, zl = n // 4, (n // 2) % 2, n % 2
        row0 = tile_row(xq, zh)
        place_rows(lambda y, rg: recv[n * 4 + y, 0, pl.ds(rg * 8, 8), :], nat, zl, row0, False)
        place_rows(
            lambda y, rg: recv[n * 4 + y, 1, pl.ds(rg * 8, 8), :], natv, zl * 2 + core, row0, True
        )
        place_rows(
            lambda y, rg: vel_other[n * 4 + y, pl.ds(rg * 8, 8), :],
            natv,
            zl * 2 + 1 - core,
            row0,
            True,
        )

    @pl.loop(0, 2)
    def _(zl):
        row0 = jnp.where(half == 0, 128, 0)
        place_rows(lambda y, rg: halo[zl * 4 + y, 0, pl.ds(rg * 8, 8), :], nat, zl, row0, False)
        place_rows(
            lambda y, rg: halo[zl * 4 + y, 1, pl.ds(rg * 8, 8), :], natv, zl * 2 + core, row0, True
        )
        place_rows(
            lambda y, rg: halo_vel_other[zl * 4 + y, pl.ds(rg * 8, 8), :],
            natv,
            zl * 2 + 1 - core,
            row0,
            True,
        )

    for part in range(2):
        for i in range(BLK):
            for v in range(4):
                term[0, part, i, v] = nat[part, v, pl.ds(i, 8, stride=BLK), :]

    def across(x):
        right = jnp.where(last, 0.0, pltpu.roll(x[0], 127, 1))
        left = jnp.where(first, 0.0, pltpu.roll(x[3], 1, 1))
        q = [x[0] + x[1], x[1] + x[2], x[2] + x[3]]
        return [(left + x[0]) + q[0], q[0] + q[1], q[1] + q[2], q[2] + (x[3] + right)]

    def apply(part, source, finish):
        def row(i):
            return [term[source, part, i, v] for v in range(4)]

        h_low = [jnp.where(sub == 0, 0.0, pltpu.roll(h, 1, 0)) for h in across(row(BLK - 1))]
        h_cur = across(row(0))
        h_high = [jnp.where(sub == 7, 0.0, pltpu.roll(h, 7, 0)) for h in h_cur]
        pair = [a + b for a, b in zip(h_low, h_cur)]
        for i in range(BLK):
            h_next = across(row(i + 1)) if i < BLK - 1 else h_high
            pair_next = [a + b for a, b in zip(h_cur, h_next)]
            for v in range(4):
                finish(i, v, pair[v] + pair_next[v])
            pair, h_cur = pair_next, h_next

    @pl.loop(0, DEPTHS)
    def _(depth):
        for part in range(2):

            def first_term(i, v, s):
                term[1, part, i, v] = 0.125 * s - term[0, part, i, v]

            apply(part, 0, first_term)

        @pl.loop(1, TOP)
        def _(k):
            for part in range(2):

                def next_term(i, v, s):
                    cur = term[k, part, i, v]
                    term[k + 1, part, i, v] = (0.25 * s - cur) - (cur + term[k - 1, part, i, v])

                apply(part, k, next_term)

        @pl.loop(0, BLK)
        def _(i):
            for v in range(4):
                idx = natv[depth, v, pl.ds(i, 8, stride=BLK), :]
                real = imag = None
                for k in range(TOP + 1):
                    c_re = jnp.take_along_axis(table[2 * k], idx, axis=1, mode="promise_in_bounds")
                    c_im = jnp.take_along_axis(
                        table[2 * k + 1], idx, axis=1, mode="promise_in_bounds"
                    )
                    t_re = term[k, 0, i, v]
                    t_im = term[k, 1, i, v]
                    re = c_re * t_re - c_im * t_im
                    im = c_re * t_im + c_im * t_re
                    real = re if real is None else real + re
                    imag = im if imag is None else imag + im
                term[0, 0, i, v] = real
                term[0, 1, i, v] = imag
                img[v, pl.ds(i, 8, stride=BLK), :] = real

        slot = jnp.where(depth % 2 == core, 0, 1)
        zl = depth // 2

        @pl.loop(0, 4)
        def _(n):
            xq, zh = n // 2, n % 2
            row0 = tile_row(xq, zh)
            for rg in range(4):
                vals = [
                    img[v, pl.ds(pl.multiple_of(row0 + rg * 8, 8), 8), :] for v in range(4)
                ]
                for y in range(4):
                    idx = 32 * y + lane // 4
                    got = [
                        jnp.take_along_axis(c, idx, axis=1, mode="promise_in_bounds") for c in vals
                    ]
                    rem = lane % 4
                    res = jnp.where(
                        rem < 2,
                        jnp.where(rem == 0, got[0], got[1]),
                        jnp.where(rem == 2, got[2], got[3]),
                    )
                    out[slot, (n * 2 + zl) * 4 + y, pl.ds(rg * 8, 8), :] = res


def extrapolate(place, recv, halo, vel_other, halo_vel_other, table):
    vmem = pl.BlockSpec(memory_space=pltpu.VMEM)
    return pl.pallas_call(
        kernel,
        out_shape=jax.ShapeDtypeStruct((2, 32, 32, 128), jnp.float32),
        in_specs=[pl.BlockSpec(memory_space=pltpu.SMEM)] + [vmem] * 5,
        out_specs=vmem,
        scratch_shapes=[
            pltpu.VMEM((2, 4, ROWS, 128), jnp.float32),
            pltpu.VMEM((DEPTHS, 4, ROWS, 128), jnp.int32),
            pltpu.VMEM((TOP + 1, 2, BLK, 4, 8, 128), jnp.float32),
            pltpu.VMEM((4, ROWS, 128), jnp.float32),
        ],
        compiler_params=pltpu.CompilerParams(vmem_limit_bytes=40 * 1024 * 1024),
        cost_estimate=pl.CostEstimate(flops=70_000_000, bytes_accessed=4_000_000, transcendentals=0),
    )(place, recv, halo, vel_other, halo_vel_other, table)


def per_device(surface, coef_table, vel_index):
    sec = lax.axis_index("sec")
    gx = lax.axis_index("gx")
    gy = lax.axis_index("gy")
    zl, core = sec // 2, sec % 2
    x, zh = gx // 2, gx % 2
    half = x // 2
    xq = jnp.where(half == 0, x, 3 - x)
    freq = core * 32 + ((xq * 2 + zh) * 2 + zl) * 4 + gy
    place = jnp.stack([half, core]).astype(jnp.int32)

    with jax.named_scope("pack"):
        mine = lax.dynamic_slice(surface, (core * 32, zl, 0, 0), (32, 1, 32, 128))
        vel = jnp.broadcast_to(vel_index.astype(jnp.float32)[None], (32, 1, 32, 128))
        send = jnp.concatenate([mine, vel], axis=1)
        table = lax.dynamic_slice(coef_table, (freq, 0, 0, 0), (1, TOP + 1, 2, NV))
        table = jnp.pad(table.reshape(2 * (TOP + 1), 1, NV), ((0, 0), (0, 0), (0, 128 - NV)))
        table = jnp.broadcast_to(table, (2 * (TOP + 1), 8, 128))
    with jax.named_scope("spread"):
        recv = lax.all_to_all(send, AXES, 0, 0, axis_index_groups=groups_of_half())
    with jax.named_scope("halo"):
        edge = lax.dynamic_slice(
            recv.reshape(2, 2, 8, 2, 32, 128), (1, 1 - half, 0, 0, 0, 0), (1, 1, 8, 2, 32, 128)
        ).reshape(8, 2, 32, 128)
        halo = lax.ppermute(edge, AXES, half_pairs())
    with jax.named_scope("velocity"):
        vel_other = lax.ppermute(recv[:, 1], AXES, core_pairs())
        halo_vel_other = lax.ppermute(halo[:, 1], AXES, core_pairs())
    with jax.named_scope("extrapolate"):
        out = extrapolate(place, recv, halo, vel_other, halo_vel_other, table)
    with jax.named_scope("image"):
        total = out[0] + lax.ppermute(out[1], AXES, core_pairs())
        parts = lax.all_to_all(total, AXES, 0, 0, axis_index_groups=groups_of_half())
        return jnp.sum(parts, axis=0, keepdims=True)


def solution(mesh):
    in_specs = (P(None, None, "gx", "gy"), P(), P("sec", "gx", "gy"))
    out_specs = P("sec", "gx", "gy")
    return jax.shard_map(
        per_device, mesh=mesh, in_specs=in_specs, out_specs=out_specs, check_vma=False
    )
```

```python
import jax
import jax.numpy as jnp
from jax import lax
from jax.experimental import pallas as pl
from jax.experimental.pallas import tpu as pltpu
from jax.sharding import PartitionSpec as P

AXES = ("sec", "gx", "gy")
ROWS = 160
BLK = 20
TOP = 8
DEPTHS = 4
NV = 64
COEFS = 2 * (TOP + 1)


def flat(x, y, zh, zl, core):
    return ((zl * 2 + core) * 8 + x * 2 + zh) * 4 + y


def half_x(half, xq):
    return xq if half == 0 else 3 - xq


def groups_of_half():
    return [
        [
            flat(half_x(half, xq), y, zh, zl, core)
            for xq in range(2)
            for zh in range(2)
            for zl in range(2)
            for y in range(4)
        ]
        for half in range(2)
        for core in range(2)
    ]


def all_devices():
    for x in range(4):
        for y in range(4):
            for zh in range(2):
                for zl in range(2):
                    for core in range(2):
                        yield x, y, zh, zl, core


def core_pairs():
    return [(flat(*d), flat(*d[:4], 1 - d[4])) for d in all_devices()]


def half_pairs():
    return [(flat(*d), flat(3 - d[0], *d[1:])) for d in all_devices()]


def gather_lanes(x, idx):
    return jnp.take_along_axis(x, idx, axis=1, mode="promise_in_bounds")


def lanes():
    return lax.broadcasted_iota(jnp.int32, (8, 128), 1)


def swap_blocks(x):
    lane = lanes()
    low = lane < 64
    even = (lane // 32) % 2 == 0
    near = [jnp.where(low, x[i], pltpu.roll(x[i + 2], 64, 1)) for i in range(2)]
    far = [jnp.where(low, pltpu.roll(x[i], 64, 1), x[i + 2]) for i in range(2)]
    res = []
    for a, b in (near, far):
        res.append(jnp.where(even, a, pltpu.roll(b, 32, 1)))
        res.append(jnp.where(even, pltpu.roll(a, 96, 1), b))
    return res


def coordinates():
    sec, gx = lax.axis_index("sec"), lax.axis_index("gx")
    x, zh = gx // 2, gx % 2
    return x, zh, sec // 2, sec % 2


def pack_kernel(surface, vel, send, buf, vel_buf, sems):
    _, _, zl, core = coordinates()
    lane = lanes()
    idx = 4 * (lane % 32) + lane // 32
    vel_copy = pltpu.make_async_copy(vel, vel_buf, sems.at[4])
    vel_copy.start()
    copies = [
        pltpu.make_async_copy(
            surface.at[pl.ds(core * 32 + j * 8, 8), zl], buf.at[pl.ds(j * 8, 8)], sems.at[j]
        )
        for j in range(4)
    ]
    for copy in copies:
        copy.start()
    vel_copy.wait()
    rows = [
        gather_lanes(vel_buf[0, pl.ds(rg * 8, 8), :].astype(jnp.float32), idx) for rg in range(4)
    ]

    @pl.loop(0, 32)
    def _(n):
        for rg in range(4):
            send[n, 1, pl.ds(rg * 8, 8), :] = rows[rg]

    for j, copy in enumerate(copies):
        copy.wait()

        @pl.loop(0, 2)
        def _(m):
            for u in range(4):
                n = j * 8 + m * 4 + u
                for rg in range(4):
                    send[n, 0, pl.ds(rg * 8, 8), :] = gather_lanes(
                        buf[n, pl.ds(rg * 8, 8), :], idx
                    )


def pack(surface, vel):
    vmem = pl.BlockSpec(memory_space=pltpu.VMEM)
    return pl.pallas_call(
        pack_kernel,
        out_shape=jax.ShapeDtypeStruct((32, 2, 32, 128), jnp.float32),
        in_specs=[pl.BlockSpec(memory_space=pl.ANY)] * 2,
        out_specs=vmem,
        scratch_shapes=[
            pltpu.VMEM((32, 32, 128), jnp.float32),
            pltpu.VMEM((1, 32, 128), jnp.int32),
            pltpu.SemaphoreType.DMA((5,)),
        ],
        compiler_params=pltpu.CompilerParams(vmem_limit_bytes=60 * 1024 * 1024),
    )(surface, vel)


def sum_kernel(parts, image):
    lane = lanes()
    idx = 32 * (lane % 4) + lane // 4
    for rg in range(4):
        terms = [parts[n, pl.ds(rg * 8, 8), :] for n in range(32)]
        while len(terms) > 1:
            terms = [a + b for a, b in zip(terms[::2], terms[1::2])]
        image[0, pl.ds(rg * 8, 8), :] = gather_lanes(terms[0], idx)


def add_up(parts):
    vmem = pl.BlockSpec(memory_space=pltpu.VMEM)
    return pl.pallas_call(
        sum_kernel,
        out_shape=jax.ShapeDtypeStruct((1, 32, 128), jnp.float32),
        in_specs=[vmem],
        out_specs=vmem,
        compiler_params=pltpu.CompilerParams(vmem_limit_bytes=16 * 1024 * 1024),
    )(parts)


def kernel(
    recv, halo, halo_vel, vel_other, halo_vel_other, table, out, nat, natv, term, img
):
    x, _, _, core = coordinates()
    half = x // 2
    lane = lanes()
    sub = lax.broadcasted_iota(jnp.int32, (8, 128), 0)
    first = lane == 0
    last = lane == 127

    def place_rows(load, dst, lead, row0, convert):
        for rg in range(4):
            vs = swap_blocks([load(y, rg) for y in range(4)])
            for v in range(4):
                val = vs[v].astype(jnp.int32) if convert else vs[v]
                dst[lead, v, pl.ds(pl.multiple_of(row0 + rg * 8, 8), 8), :] = val

    def tile_row(xq, zh):
        return jnp.where(half == 0, 2 * xq + zh, 3 - 2 * xq + zh) * 32

    @pl.loop(0, 8)
    def _(n):
        xq, zh, zl = n // 4, (n // 2) % 2, n % 2
        row0 = tile_row(xq, zh)
        place_rows(lambda y, rg: recv[n * 4 + y, 0, pl.ds(rg * 8, 8), :], nat, zl, row0, False)
        place_rows(
            lambda y, rg: recv[n * 4 + y, 1, pl.ds(rg * 8, 8), :], natv, zl * 2 + core, row0, True
        )
        place_rows(
            lambda y, rg: vel_other[n * 4 + y, pl.ds(rg * 8, 8), :],
            natv,
            zl * 2 + 1 - core,
            row0,
            True,
        )

    edge = jnp.where(half == 0, 128, 0)
    natv[:, :, pl.ds(pl.multiple_of(edge, 8), 32), :] = jnp.zeros((DEPTHS, 4, 32, 128), jnp.int32)
    for part in range(2):
        place_rows(lambda y, rg: halo[part * 4 + y, pl.ds(rg * 8, 8), :], nat, part, edge, False)

    for ref, parity in ((halo_vel, core), (halo_vel_other, 1 - core)):
        for rg in range(4):
            vs = swap_blocks([ref[y, pl.ds(rg * 8, 8), :] for y in range(4)])
            first_row = jnp.where(half == 0, 128, 8) + rg * 8
            row0 = first_row if rg < 3 else jnp.where(half == 0, 128, 24)
            depth = parity if rg < 3 else 2 + parity
            for v in range(4):
                natv[depth, v, pl.ds(pl.multiple_of(row0, 8), 8), :] = vs[v].astype(jnp.int32)

    for part in range(2):
        for i in range(BLK):
            for v in range(4):
                term[0, part, i, v] = nat[part, v, pl.ds(i, 8, stride=BLK), :]

    def across(x):
        right = jnp.where(last, 0.0, pltpu.roll(x[0], 127, 1))
        left = jnp.where(first, 0.0, pltpu.roll(x[3], 1, 1))
        q = [x[0] + x[1], x[1] + x[2], x[2] + x[3]]
        return [(left + x[0]) + q[0], q[0] + q[1], q[1] + q[2], q[2] + (x[3] + right)]

    def apply(part, source, finish):
        def row(i):
            return [term[source, part, i, v] for v in range(4)]

        h_low = [jnp.where(sub == 0, 0.0, pltpu.roll(h, 1, 0)) for h in across(row(BLK - 1))]
        h_cur = across(row(0))
        h_high = [jnp.where(sub == 7, 0.0, pltpu.roll(h, 7, 0)) for h in h_cur]
        pair = [a + b for a, b in zip(h_low, h_cur)]
        for i in range(BLK):
            h_next = across(row(i + 1)) if i < BLK - 1 else h_high
            pair_next = [a + b for a, b in zip(h_cur, h_next)]
            for v in range(4):
                finish(i, v, pair[v] + pair_next[v])
            pair, h_cur = pair_next, h_next

    @pl.loop(0, DEPTHS)
    def _(depth):
        for part in range(2):

            def first_term(i, v, s):
                term[1, part, i, v] = 0.125 * s - term[0, part, i, v]

            apply(part, 0, first_term)

        @pl.loop(1, TOP)
        def _(k):
            for part in range(2):

                def next_term(i, v, s):
                    cur = term[k, part, i, v]
                    term[k + 1, part, i, v] = (0.25 * s - cur) - (cur + term[k - 1, part, i, v])

                apply(part, k, next_term)

        @pl.loop(0, BLK, unroll=10)
        def _(i):
            for v in range(4):
                idx = natv[depth, v, pl.ds(i, 8, stride=BLK), :]
                real = imag = None
                for k in range(TOP + 1):
                    c_re = gather_lanes(table[2 * k], idx)
                    c_im = gather_lanes(table[2 * k + 1], idx)
                    t_re = term[k, 0, i, v]
                    t_im = term[k, 1, i, v]
                    re = c_re * t_re - c_im * t_im
                    im = c_re * t_im + c_im * t_re
                    real = re if real is None else real + re
                    imag = im if imag is None else imag + im
                term[0, 0, i, v] = real
                term[0, 1, i, v] = imag
                img[v, pl.ds(i, 8, stride=BLK), :] = real

        slot = jnp.where(depth % 2 == core, 0, 1)
        zl = depth // 2

        @pl.loop(0, 4, unroll=4)
        def _(n):
            xq, zh = n // 2, n % 2
            row0 = tile_row(xq, zh)
            for rg in range(4):
                vals = swap_blocks(
                    [img[v, pl.ds(pl.multiple_of(row0 + rg * 8, 8), 8), :] for v in range(4)]
                )
                for y in range(4):
                    out[slot, (n * 2 + zl) * 4 + y, pl.ds(rg * 8, 8), :] = vals[y]


def extrapolate(*operands):
    vmem = pl.BlockSpec(memory_space=pltpu.VMEM)
    return pl.pallas_call(
        kernel,
        out_shape=jax.ShapeDtypeStruct((2, 32, 32, 128), jnp.float32),
        in_specs=[vmem] * 6,
        out_specs=vmem,
        scratch_shapes=[
            pltpu.VMEM((2, 4, ROWS, 128), jnp.float32),
            pltpu.VMEM((DEPTHS, 4, ROWS, 128), jnp.int32),
            pltpu.VMEM((TOP + 1, 2, BLK, 4, 8, 128), jnp.float32),
            pltpu.VMEM((4, ROWS, 128), jnp.float32),
        ],
        compiler_params=pltpu.CompilerParams(vmem_limit_bytes=40 * 1024 * 1024),
        cost_estimate=pl.CostEstimate(flops=70_000_000, bytes_accessed=4_000_000, transcendentals=0),
    )(*operands)


def per_device(surface, coef_table, vel_index):
    sec = lax.axis_index("sec")
    gx = lax.axis_index("gx")
    gy = lax.axis_index("gy")
    zl, core = sec // 2, sec % 2
    x, zh = gx // 2, gx % 2
    half = x // 2
    xq = jnp.where(half == 0, x, 3 - x)
    freq = core * 32 + ((xq * 2 + zh) * 2 + zl) * 4 + gy

    with jax.named_scope("pack"):
        send = pack(surface, vel_index)
    with jax.named_scope("spread"):
        recv = lax.all_to_all(send, AXES, 0, 0, axis_index_groups=groups_of_half())
    with jax.named_scope("halo"):
        edge = lax.dynamic_slice(
            recv.reshape(2, 2, 8, 2, 32, 128), (1, 1 - half, 0, 0, 0, 0), (1, 1, 8, 2, 32, 128)
        ).reshape(8, 2, 32, 128)
        edge_vel = jnp.concatenate(
            [
                lax.dynamic_slice(edge, (0, 1, 8 * (1 - half), 0), (4, 1, 24, 128))[:, 0],
                lax.dynamic_slice(edge, (4, 1, 24 * (1 - half), 0), (4, 1, 8, 128))[:, 0],
            ],
            axis=1,
        )
        halo_vel = lax.ppermute(edge_vel, AXES, half_pairs())
        halo = lax.ppermute(edge[:, 0], AXES, half_pairs())
    with jax.named_scope("velocity"):
        vel_other = lax.ppermute(recv[:, 1], AXES, core_pairs())
        halo_vel_other = lax.ppermute(halo_vel, AXES, core_pairs())
    with jax.named_scope("tables"):
        own = lax.dynamic_slice(coef_table, (freq, 0, 0, 0), (1, TOP + 1, 2, NV))
        own = own.reshape(COEFS, NV)
        table = jnp.pad(own[:, None], ((0, 0), (0, 0), (0, 128 - NV)))
        table = jnp.broadcast_to(table, (COEFS, 8, 128))
    with jax.named_scope("extrapolate"):
        out = extrapolate(recv, halo, halo_vel, vel_other, halo_vel_other, table)
    with jax.named_scope("image"):
        total = out[0] + lax.ppermute(out[1], AXES, core_pairs())
        parts = lax.all_to_all(total, AXES, 0, 0, axis_index_groups=groups_of_half())
        return add_up(parts)


def solution(mesh):
    in_specs = (P(None, None, "gx", "gy"), P(), P("sec", "gx", "gy"))
    out_specs = P("sec", "gx", "gy")
    return jax.shard_map(
        per_device, mesh=mesh, in_specs=in_specs, out_specs=out_specs, check_vma=False
    )
```

```python
import jax
import jax.numpy as jnp
from jax import lax
from jax.experimental import pallas as pl
from jax.experimental.pallas import tpu as pltpu
from jax.sharding import PartitionSpec as P

AXES = ("sec", "gx", "gy")
OWN = 16
BLK = 20
PITCH = 24
AHEAD = 3
TOP = 8
DEPTHS = 4
NV = 64
COEFS = 2 * (TOP + 1)


def flat(x, y, zh, zl, core):
    return ((zl * 2 + core) * 8 + x * 2 + zh) * 4 + y


def half_x(half, xq):
    return xq if half == 0 else 3 - xq


def groups_of_half():
    return [
        [
            flat(half_x(half, xq), y, zh, zl, core)
            for xq in range(2)
            for zh in range(2)
            for zl in range(2)
            for y in range(4)
        ]
        for half in range(2)
        for core in range(2)
    ]


def all_devices():
    for x in range(4):
        for y in range(4):
            for zh in range(2):
                for zl in range(2):
                    for core in range(2):
                        yield x, y, zh, zl, core


def core_pairs():
    return [(flat(*d), flat(*d[:4], 1 - d[4])) for d in all_devices()]


def half_pairs():
    return [(flat(*d), flat(3 - d[0], *d[1:])) for d in all_devices()]


def gather_lanes(x, idx):
    return jnp.take_along_axis(x, idx, axis=1, mode="promise_in_bounds")


def lanes():
    return lax.broadcasted_iota(jnp.int32, (8, 128), 1)


def swap_blocks(x):
    lane = lanes()
    low = lane < 64
    even = (lane // 32) % 2 == 0
    near = [jnp.where(low, x[i], pltpu.roll(x[i + 2], 64, 1)) for i in range(2)]
    far = [jnp.where(low, pltpu.roll(x[i], 64, 1), x[i + 2]) for i in range(2)]
    res = []
    for a, b in (near, far):
        res.append(jnp.where(even, a, pltpu.roll(b, 32, 1)))
        res.append(jnp.where(even, pltpu.roll(a, 96, 1), b))
    return res


def coordinates():
    sec, gx = lax.axis_index("sec"), lax.axis_index("gx")
    x, zh = gx // 2, gx % 2
    return x, zh, sec // 2, sec % 2


def pack_kernel(surface, vel, send, buf, vel_buf, sems):
    _, _, zl, core = coordinates()
    lane = lanes()
    idx = 4 * (lane % 32) + lane // 32
    vel_copy = pltpu.make_async_copy(vel, vel_buf, sems.at[4])
    vel_copy.start()
    copies = [
        pltpu.make_async_copy(
            surface.at[pl.ds(core * 32 + j * 8, 8), zl], buf.at[pl.ds(j * 8, 8)], sems.at[j]
        )
        for j in range(4)
    ]
    for copy in copies:
        copy.start()
    vel_copy.wait()
    rows = [
        gather_lanes(vel_buf[0, pl.ds(rg * 8, 8), :].astype(jnp.float32), idx) for rg in range(4)
    ]

    for n in range(32):
        for rg in range(4):
            send[n, 1, pl.ds(rg * 8, 8), :] = rows[rg]

    for j, copy in enumerate(copies):
        copy.wait()
        for u in range(8):
            n = j * 8 + u
            for rg in range(4):
                send[n, 0, pl.ds(rg * 8, 8), :] = gather_lanes(buf[n, pl.ds(rg * 8, 8), :], idx)


def pack(surface, vel):
    vmem = pl.BlockSpec(memory_space=pltpu.VMEM)
    return pl.pallas_call(
        pack_kernel,
        out_shape=jax.ShapeDtypeStruct((32, 2, 32, 128), jnp.float32),
        in_specs=[pl.BlockSpec(memory_space=pl.ANY)] * 2,
        out_specs=vmem,
        scratch_shapes=[
            pltpu.VMEM((32, 32, 128), jnp.float32),
            pltpu.VMEM((1, 32, 128), jnp.int32),
            pltpu.SemaphoreType.DMA((5,)),
        ],
        compiler_params=pltpu.CompilerParams(vmem_limit_bytes=60 * 1024 * 1024),
    )(surface, vel)


def sum_kernel(parts, image):
    lane = lanes()
    idx = 32 * (lane % 4) + lane // 4
    for rg in range(4):
        terms = [parts[n, pl.ds(rg * 8, 8), :] for n in range(32)]
        while len(terms) > 1:
            terms = [a + b for a, b in zip(terms[::2], terms[1::2])]
        image[0, pl.ds(rg * 8, 8), :] = gather_lanes(terms[0], idx)


def add_up(parts):
    vmem = pl.BlockSpec(memory_space=pltpu.VMEM)
    return pl.pallas_call(
        sum_kernel,
        out_shape=jax.ShapeDtypeStruct((1, 32, 128), jnp.float32),
        in_specs=[vmem],
        out_specs=vmem,
        compiler_params=pltpu.CompilerParams(vmem_limit_bytes=16 * 1024 * 1024),
    )(parts)


def tile_group(t, rg):
    return pl.ds(pl.multiple_of((2 * t + rg // 2) * PITCH + 8 * (rg % 2), 8), 8)


def own_tile(half, n):
    return jnp.where(half == 0, n, (n + 2) % 4)


def prepare_kernel(recv, vel_other, table, start, index, coefs, zero, nat, natv):
    zero[...] = jnp.zeros_like(zero)
    x, _, _, core = coordinates()
    half = x // 2

    @pl.loop(0, 8)
    def _(n):
        t = own_tile(half, n // 2)
        zl = n % 2
        for rg in range(4):
            dst = tile_group(t, rg)
            for slab in range(2):
                vs = swap_blocks([recv[n * 4 + y, slab, pl.ds(rg * 8, 8), :] for y in range(4)])
                for v in range(4):
                    if slab == 0:
                        nat[zl, v, dst, :] = vs[v]
                    else:
                        natv[zl * 2 + core, v, dst, :] = vs[v].astype(jnp.int32)
            vs = swap_blocks([vel_other[n * 4 + y, pl.ds(rg * 8, 8), :] for y in range(4)])
            for v in range(4):
                natv[zl * 2 + 1 - core, v, dst, :] = vs[v].astype(jnp.int32)

    def block(i):
        return pl.ds(i, 8, stride=PITCH)

    for i in range(OWN):
        for v in range(4):
            for part in range(2):
                start[part, i, v] = nat[part, v, block(i), :]
            for depth in range(AHEAD, DEPTHS):
                index[depth - AHEAD, i, v] = natv[depth, v, block(i), :]

    @pl.loop(0, AHEAD)
    def _(depth):
        @pl.loop(0, OWN, unroll=8)
        def _(i):
            for v in range(4):
                idx = natv[depth, v, block(i), :]
                for n in range(COEFS):
                    coefs[depth, i, v, n] = gather_lanes(table[n], idx)


def prepare(recv, vel_other, table):
    vmem = pl.BlockSpec(memory_space=pltpu.VMEM)
    return pl.pallas_call(
        prepare_kernel,
        out_shape=(
            jax.ShapeDtypeStruct((2, OWN, 4, 8, 128), jnp.float32),
            jax.ShapeDtypeStruct((DEPTHS - AHEAD, OWN, 4, 8, 128), jnp.int32),
            jax.ShapeDtypeStruct((AHEAD, OWN, 4, COEFS, 8, 128), jnp.float32),
            jax.ShapeDtypeStruct((8, 128), jnp.float32),
        ),
        in_specs=[vmem] * 3,
        out_specs=(vmem,) * 4,
        scratch_shapes=[
            pltpu.VMEM((2, 4, 8 * PITCH, 128), jnp.float32),
            pltpu.VMEM((DEPTHS, 4, 8 * PITCH, 128), jnp.int32),
        ],
        compiler_params=pltpu.CompilerParams(vmem_limit_bytes=24 * 1024 * 1024),
        cost_estimate=pl.CostEstimate(flops=20_000_000, bytes_accessed=4_000_000, transcendentals=0),
    )(recv, vel_other, table)


def kernel(start, index, coefs, halo, halo_vel_other, table, out, nat, natv, term, img):
    x, _, _, core = coordinates()
    half = x // 2
    lane = lanes()
    sub = lax.broadcasted_iota(jnp.int32, (8, 128), 0)
    first = lane == 0
    last = lane == 127
    before = jnp.where(half == 0, 0.0, 1.0)
    after = 1.0 - before

    for part in range(2):
        for rg in range(4):
            vs = swap_blocks([halo[part * 4 + y, pl.ds(rg * 8, 8), :] for y in range(4)])
            for v in range(4):
                nat[part, v, pl.ds(rg * 8, 8), :] = vs[v]

    natv[...] = jnp.zeros_like(natv)
    for ref, parity in ((halo.at[pl.ds(8, 4)], core), (halo_vel_other, 1 - core)):
        for rg in range(4):
            vs = swap_blocks([ref[y, pl.ds(rg * 8, 8), :] for y in range(4)])
            if rg < 3:
                row0, depth = jnp.where(half == 0, 0, 8) + rg * 8, parity
            else:
                row0, depth = jnp.where(half == 0, 0, 24), 2 + parity
            for v in range(4):
                natv[depth, v, pl.ds(pl.multiple_of(row0, 8), 8), :] = vs[v].astype(jnp.int32)

    for part in range(2):
        for i in range(OWN):
            for v in range(4):
                term[0, part, i, v] = start[part, i, v]
        for j in range(BLK - OWN):
            for v in range(4):
                term[0, part, OWN + j, v] = nat[part, v, pl.ds(j, 8, stride=4), :]

    def across(x):
        right = jnp.where(last, 0.0, pltpu.roll(x[0], 127, 1))
        left = jnp.where(first, 0.0, pltpu.roll(x[3], 1, 1))
        q = [x[0] + x[1], x[1] + x[2], x[2] + x[3]]
        return [(left + x[0]) + q[0], q[0] + q[1], q[1] + q[2], q[2] + (x[3] + right)]

    def apply(part, source, finish):
        def row(i):
            return across([term[source, part, i, v] for v in range(4)])

        down = {i: [pltpu.roll(h, 1, 0) for h in row(i)] for i in (OWN - 1, BLK - 1)}
        h_own, h_halo = row(0), row(OWN)
        up = {0: [pltpu.roll(h, 7, 0) for h in h_own], OWN: [pltpu.roll(h, 7, 0) for h in h_halo]}

        def ends(at, other, flag, same):
            return [
                jnp.where(sub == at, flag * a, b) for a, b in zip(other, same)
            ]

        chains = (
            (
                range(OWN),
                h_own,
                ends(0, down[BLK - 1], before, down[OWN - 1]),
                ends(7, up[OWN], after, up[0]),
            ),
            (
                range(OWN, BLK),
                h_halo,
                ends(0, down[OWN - 1], after, down[BLK - 1]),
                ends(7, up[0], before, up[OWN]),
            ),
        )
        for span, h_cur, h_low, h_high in chains:
            pair = [a + b for a, b in zip(h_low, h_cur)]
            for i in span:
                h_next = row(i + 1) if i < span[-1] else h_high
                pair_next = [a + b for a, b in zip(h_cur, h_next)]
                for v in range(4):
                    finish(i, v, pair[v] + pair_next[v])
                pair, h_cur = pair_next, h_next

    def combine(i, v, coef):
        real = imag = None
        for k in range(TOP + 1):
            c_re, c_im = coef(2 * k), coef(2 * k + 1)
            t_re = term[k, 0, i, v]
            t_im = term[k, 1, i, v]
            re = c_re * t_re - c_im * t_im
            im = c_re * t_im + c_im * t_re
            real = re if real is None else real + re
            imag = im if imag is None else imag + im
        term[0, 0, i, v] = real
        term[0, 1, i, v] = imag
        return real

    @pl.loop(0, DEPTHS)
    def _(depth):
        for part in range(2):

            def first_term(i, v, s):
                term[1, part, i, v] = 0.125 * s - term[0, part, i, v]

            apply(part, 0, first_term)

        @pl.loop(1, TOP)
        def _(k):
            for part in range(2):

                def next_term(i, v, s):
                    cur = term[k, part, i, v]
                    term[k + 1, part, i, v] = (0.25 * s - cur) - (cur + term[k - 1, part, i, v])

                apply(part, k, next_term)

        @pl.when(depth < AHEAD)
        def _():
            @pl.loop(0, OWN, unroll=4)
            def _(i):
                for v in range(4):
                    img[v, pl.ds(i, 8, stride=PITCH), :] = combine(
                        i, v, lambda n: coefs[depth, i, v, n]
                    )

        @pl.when(depth >= AHEAD)
        def _():
            @pl.loop(0, OWN, unroll=8)
            def _(i):
                for v in range(4):
                    idx = index[depth - AHEAD, i, v]
                    img[v, pl.ds(i, 8, stride=PITCH), :] = combine(
                        i, v, lambda n: gather_lanes(table[n], idx)
                    )

        @pl.when(depth < DEPTHS - 1)
        def _():
            for j in range(BLK - OWN):
                for v in range(4):
                    idx = natv[depth, v, pl.ds(j, 8, stride=4), :]
                    combine(OWN + j, v, lambda n: gather_lanes(table[n], idx))

        slot = jnp.where(depth % 2 == core, 0, 1)
        zl = depth // 2

        @pl.loop(0, 4, unroll=4)
        def _(n):
            t = own_tile(half, n)
            for rg in range(4):
                vals = swap_blocks([img[v, tile_group(t, rg), :] for v in range(4)])
                for y in range(4):
                    out[slot, (n * 2 + zl) * 4 + y, pl.ds(rg * 8, 8), :] = vals[y]


def extrapolate(*operands):
    vmem = pl.BlockSpec(memory_space=pltpu.VMEM)
    return pl.pallas_call(
        kernel,
        out_shape=jax.ShapeDtypeStruct((2, 32, 32, 128), jnp.float32),
        in_specs=[vmem] * 6,
        out_specs=vmem,
        scratch_shapes=[
            pltpu.VMEM((2, 4, 32, 128), jnp.float32),
            pltpu.VMEM((DEPTHS, 4, 32, 128), jnp.int32),
            pltpu.VMEM((TOP + 1, 2, BLK, 4, 8, 128), jnp.float32),
            pltpu.VMEM((4, 8 * PITCH, 128), jnp.float32),
        ],
        compiler_params=pltpu.CompilerParams(vmem_limit_bytes=28 * 1024 * 1024),
        cost_estimate=pl.CostEstimate(flops=70_000_000, bytes_accessed=4_000_000, transcendentals=0),
    )(*operands)


def per_device(surface, coef_table, vel_index):
    sec = lax.axis_index("sec")
    gx = lax.axis_index("gx")
    gy = lax.axis_index("gy")
    zl, core = sec // 2, sec % 2
    x, zh = gx // 2, gx % 2
    half = x // 2
    xq = jnp.where(half == 0, x, 3 - x)
    freq = core * 32 + ((xq * 2 + zh) * 2 + zl) * 4 + gy

    with jax.named_scope("pack"):
        send = pack(surface, vel_index)
    with jax.named_scope("spread"):
        recv = lax.all_to_all(send, AXES, 0, 0, axis_index_groups=groups_of_half())
    with jax.named_scope("halo"):
        edge = lax.dynamic_slice(
            recv.reshape(2, 2, 8, 2, 32, 128), (1, 1 - half, 0, 0, 0, 0), (1, 1, 8, 2, 32, 128)
        ).reshape(8, 2, 32, 128)
        edge_vel = jnp.concatenate(
            [
                lax.dynamic_slice(edge, (0, 1, 8 * (1 - half), 0), (4, 1, 24, 128))[:, 0],
                lax.dynamic_slice(edge, (4, 1, 24 * (1 - half), 0), (4, 1, 8, 128))[:, 0],
            ],
            axis=1,
        )
        halo = lax.ppermute(
            jnp.concatenate([edge[:, 0], edge_vel], axis=0), AXES, half_pairs()
        )
    with jax.named_scope("velocity"):
        vel_other = lax.ppermute(recv[:, 1], AXES, core_pairs())
    with jax.named_scope("tables"):
        own = lax.dynamic_slice(coef_table, (freq, 0, 0, 0), (1, TOP + 1, 2, NV))
        own = own.reshape(COEFS, NV)
        table = jnp.pad(own[:, None], ((0, 0), (0, 0), (0, 128 - NV)))
        table = jnp.broadcast_to(table, (COEFS, 8, 128))
    with jax.named_scope("prepare"):
        start, index, coefs, zero = prepare(recv, vel_other, table)
    with jax.named_scope("velocity"):
        halo_vel_other = lax.ppermute(halo[8:] + zero[:1], AXES, core_pairs())
    with jax.named_scope("extrapolate"):
        out = extrapolate(start, index, coefs, halo, halo_vel_other, table)
    with jax.named_scope("image"):
        total = out[0] + lax.ppermute(out[1], AXES, core_pairs())
        parts = lax.all_to_all(total, AXES, 0, 0, axis_index_groups=groups_of_half())
        return add_up(parts)


def solution(mesh):
    in_specs = (P(None, None, "gx", "gy"), P(), P("sec", "gx", "gy"))
    out_specs = P("sec", "gx", "gy")
    return jax.shard_map(
        per_device, mesh=mesh, in_specs=in_specs, out_specs=out_specs, check_vma=False
    )
```

```python
import jax
import jax.numpy as jnp
from jax import lax
from jax.experimental import pallas as pl
from jax.experimental.pallas import tpu as pltpu
from jax.sharding import PartitionSpec as P

AXES = ("sec", "gx", "gy")
OWN = 16
BLK = 20
PITCH = 24
WAYS = 5
AHEAD = 3
TOP = 8
DEPTHS = 4
NV = 64
COEFS = 2 * (TOP + 1)


def flat(x, y, zh, zl, core):
    return ((zl * 2 + core) * 8 + x * 2 + zh) * 4 + y


def from_rim(half, q):
    return q if half == 0 else 3 - q


def groups_of_quadrant():
    return [
        [
            flat(from_rim(half_x, xq), from_rim(half_y, yq), zh, zl, core)
            for xq in range(2)
            for zh in range(2)
            for zl in range(2)
            for yq in range(2)
        ]
        for half_x in range(2)
        for half_y in range(2)
        for core in range(2)
    ]


def pairs(partner):
    return [
        (flat(x, y, zh, zl, core), flat(*partner(x, y, zh, zl, core)))
        for x in range(4)
        for y in range(4)
        for zh in range(2)
        for zl in range(2)
        for core in range(2)
    ]


def core_pairs():
    return pairs(lambda x, y, zh, zl, core: (x, y, zh, zl, 1 - core))


def gather_lanes(x, idx):
    return jnp.take_along_axis(x, idx, axis=1, mode="promise_in_bounds")


def lanes():
    return lax.broadcasted_iota(jnp.int32, (8, 128), 1)


def rows(rg):
    return pl.ds(rg * 8, 8)


def turn(x, by):
    return pltpu.roll(x, by, 1)


def swap_blocks(x):
    lane = lanes()
    low = lane < 64
    even = (lane // 32) % 2 == 0
    near = [jnp.where(low, x[i], turn(x[i + 2], 64)) for i in range(2)]
    far = [jnp.where(low, turn(x[i], 64), x[i + 2]) for i in range(2)]
    res = []
    for a, b in (near, far):
        res.append(jnp.where(even, a, turn(b, 32)))
        res.append(jnp.where(even, turn(a, 96), b))
    return res


def coordinates():
    sec, gx, y = lax.axis_index("sec"), lax.axis_index("gx"), lax.axis_index("gy")
    x, zh = gx // 2, gx % 2
    return x, y, zh, sec // 2, sec % 2


def pack_kernel(surface, vel, send, buf, vel_buf, sems):
    _, y, _, zl, core = coordinates()
    lane = lanes()
    idx = 4 * (lane % 32) + lane // 32
    idx = jnp.where(y < 2, idx, 127 - idx)
    vel_copy = pltpu.make_async_copy(vel, vel_buf, sems.at[4])
    vel_copy.start()
    copies = [
        pltpu.make_async_copy(
            surface.at[pl.ds(core * 16 + j * 4, 4), zl], buf.at[pl.ds(j * 4, 4)], sems.at[j]
        )
        for j in range(4)
    ]
    for copy in copies:
        copy.start()
    vel_copy.wait()
    for rg in range(4):
        value = gather_lanes(vel_buf[0, rows(rg), :].astype(jnp.float32), idx)
        for n in range(16):
            send[n, 2, rows(rg), :] = value
    for j, copy in enumerate(copies):
        copy.wait()
        for n in range(j * 4, j * 4 + 4):
            for part in range(2):
                for rg in range(4):
                    send[n, part, rows(rg), :] = gather_lanes(buf[n, part, rows(rg), :], idx)


def pack(surface, vel):
    vmem = pl.BlockSpec(memory_space=pltpu.VMEM)
    return pl.pallas_call(
        pack_kernel,
        out_shape=jax.ShapeDtypeStruct((16, 3, 32, 128), jnp.float32),
        in_specs=[pl.BlockSpec(memory_space=pl.ANY)] * 2,
        out_specs=vmem,
        scratch_shapes=[
            pltpu.VMEM((16, 2, 32, 128), jnp.float32),
            pltpu.VMEM((1, 32, 128), jnp.int32),
            pltpu.SemaphoreType.DMA((5,)),
        ],
        compiler_params=pltpu.CompilerParams(vmem_limit_bytes=60 * 1024 * 1024),
    )(surface.reshape(32, 2, 2, 32, 128), vel)


def sum_kernel(parts, image):
    y = lax.axis_index("gy")
    lane = lanes()
    column = jnp.where(y < 2, lane, 127 - lane)
    idx = 32 * (column % 4) + column // 4
    for rg in range(4):
        terms = [parts[n, rows(rg), :] for n in range(16)]
        while len(terms) > 1:
            terms = [a + b for a, b in zip(terms[::2], terms[1::2])]
        image[0, rows(rg), :] = gather_lanes(terms[0], idx)


def add_up(parts):
    vmem = pl.BlockSpec(memory_space=pltpu.VMEM)
    return pl.pallas_call(
        sum_kernel,
        out_shape=jax.ShapeDtypeStruct((1, 32, 128), jnp.float32),
        in_specs=[vmem],
        out_specs=vmem,
        compiler_params=pltpu.CompilerParams(vmem_limit_bytes=16 * 1024 * 1024),
    )(parts)


def own_tile(half, n):
    return jnp.where(half == 0, n, (n + 2) % 4)


def edge_kernel(recv, own, below, beside, corner, table):
    x, _, _, _, _ = coordinates()
    half = x // 2
    lane = lanes()
    inner = lane % 32
    block = lane // 32
    last = 32 * (inner % 4) + 24 + inner // 4
    edge = 2 + (1 - half)
    for k in range(TOP + 1):
        pair = jnp.concatenate([own[0, k], own[1, k]], axis=1)
        for r in range(2):
            table[2 * k + r] = jnp.broadcast_to(pair[r : r + 1], (8, 128))

    for yq in range(2):
        for rg in range(4):
            for f in range(2):
                for part in range(2):
                    below[(f * 2 + part) * 2 + yq, rows(rg), :] = recv[
                        (edge * 2 + f) * 2 + yq, part, rows(rg), :
                    ]
            if rg < 3:
                zl, row0 = 0, 8 * (1 - half) + rg * 8
            else:
                zl, row0 = 1, 24 * (1 - half)
            below[8 + yq, rows(rg), :] = recv[
                (edge * 2 + zl) * 2 + yq, 2, pl.ds(pl.multiple_of(row0, 8), 8), :
            ]

    def final_columns(n, f, slab, rg):
        return gather_lanes(recv[(n * 2 + f) * 2 + 1, slab, rows(rg), :], last)

    for rg in range(4):
        for slab in range(3):
            a, b = [final_columns(edge, f, slab, rg) for f in range(2)]
            corner[slab, rows(rg), :] = jnp.where(lane < 64, a, b)
            for t in range(2):
                near, far = own_tile(half, t), own_tile(half, t + 2)
                a, b, c, d = [
                    final_columns(n, f, slab, rg) for f in range(2) for n in (far, near)
                ]
                beside[slab, pl.ds(t * 32 + rg * 8, 8), :] = jnp.where(
                    block < 2, jnp.where(block == 0, a, b), jnp.where(block == 2, c, d)
                )


def edges(recv, own):
    vmem = pl.BlockSpec(memory_space=pltpu.VMEM)
    return pl.pallas_call(
        edge_kernel,
        out_shape=(
            jax.ShapeDtypeStruct((10, 32, 128), jnp.float32),
            jax.ShapeDtypeStruct((3, 64, 128), jnp.float32),
            jax.ShapeDtypeStruct((3, 32, 128), jnp.float32),
            jax.ShapeDtypeStruct((COEFS, 8, 128), jnp.float32),
        ),
        in_specs=[vmem] * 2,
        out_specs=(vmem,) * 4,
        compiler_params=pltpu.CompilerParams(vmem_limit_bytes=16 * 1024 * 1024),
    )(recv, own)


def edge_velocity_kernel(below, beside, corner, zero, vel):
    for rg in range(4):
        for q in range(2):
            vel[q, rows(rg), :] = below[8 + q, rows(rg), :] + zero[...]
            vel[2 + q, rows(rg), :] = beside[2, pl.ds(q * 32 + rg * 8, 8), :]
        vel[4, rows(rg), :] = corner[2, rows(rg), :]


def edge_velocity(*operands):
    vmem = pl.BlockSpec(memory_space=pltpu.VMEM)
    return pl.pallas_call(
        edge_velocity_kernel,
        out_shape=jax.ShapeDtypeStruct((5, 32, 128), jnp.float32),
        in_specs=[vmem] * 4,
        out_specs=vmem,
        compiler_params=pltpu.CompilerParams(vmem_limit_bytes=16 * 1024 * 1024),
    )(*operands)


def tile_group(t, rg):
    return pl.ds(pl.multiple_of((2 * t + rg // 2) * PITCH + 8 * (rg % 2), 8), 8)


def prepare_kernel(recv, vel_other, table, start, index, coefs, zero, nat, natv):
    x, _, _, _, core = coordinates()
    zero[...] = jnp.zeros_like(zero)
    half = x // 2
    shift = jnp.where(lanes() < 64, 0, NV)

    @pl.loop(0, 4)
    def _(n):
        t = own_tile(half, n)
        for rg in range(4):
            dst = tile_group(t, rg)
            for part in range(2):
                vs = swap_blocks([recv[n * 4 + m, part, rows(rg), :] for m in range(4)])
                for v in range(4):
                    nat[part, v, dst, :] = vs[v]
            for zl in range(2):
                for mine in range(2):
                    two = [
                        recv[n * 4 + zl * 2 + yq, 2, rows(rg), :]
                        if mine
                        else vel_other[n * 4 + zl * 2 + yq, rows(rg), :]
                        for yq in range(2)
                    ]
                    depth = zl * 2 + (core if mine else 1 - core)
                    vs = swap_blocks(two + two)
                    for v in range(4):
                        natv[depth, v, dst, :] = vs[v].astype(jnp.int32) + shift

    def block(i):
        return pl.ds(i, 8, stride=PITCH)

    for i in range(OWN):
        for v in range(4):
            for part in range(2):
                start[part, i, v] = nat[part, v, block(i), :]
            for depth in range(AHEAD, DEPTHS):
                index[depth - AHEAD, i, v] = natv[depth, v, block(i), :]

    @pl.loop(0, AHEAD)
    def _(depth):
        @pl.loop(0, OWN, unroll=16)
        def _(i):
            for v in range(4):
                idx = natv[depth, v, block(i), :]
                for n in range(COEFS):
                    coefs[depth, i, v, n] = gather_lanes(table[n], idx)


def prepare(recv, vel_other, table):
    vmem = pl.BlockSpec(memory_space=pltpu.VMEM)
    return pl.pallas_call(
        prepare_kernel,
        out_shape=(
            jax.ShapeDtypeStruct((2, OWN, 4, 8, 128), jnp.float32),
            jax.ShapeDtypeStruct((DEPTHS - AHEAD, OWN, 4, 8, 128), jnp.int32),
            jax.ShapeDtypeStruct((AHEAD, OWN, 4, COEFS, 8, 128), jnp.float32),
            jax.ShapeDtypeStruct((8, 128), jnp.float32),
        ),
        in_specs=[vmem] * 3,
        out_specs=(vmem,) * 4,
        scratch_shapes=[
            pltpu.VMEM((2, 4, 8 * PITCH, 128), jnp.float32),
            pltpu.VMEM((DEPTHS, 4, 8 * PITCH, 128), jnp.int32),
        ],
        compiler_params=pltpu.CompilerParams(vmem_limit_bytes=24 * 1024 * 1024),
        cost_estimate=pl.CostEstimate(flops=20_000_000, bytes_accessed=4_000_000, transcendentals=0),
    )(recv, vel_other, table)


def kernel(
    start, index, coefs, below, beside, corner, vel_other, table, out,
    nat, natv, side, sidev, term, img
):
    x, _, _, _, core = coordinates()
    half = x // 2
    lane = lanes()
    sub = lax.broadcasted_iota(jnp.int32, (8, 128), 0)
    first = lane % 64 == 0
    last = lane % 64 == 63
    low = lane < 64
    shift = jnp.where(low, 0, NV)
    before = jnp.where(half == 0, 0.0, 1.0)
    after = 1.0 - before

    def block(i):
        return pl.ds(i, 8, stride=PITCH)

    for part in range(2):
        for rg in range(4):
            vs = swap_blocks(
                [below[(f * 2 + part) * 2 + yq, rows(rg), :] for f in range(2) for yq in range(2)]
            )
            for v in range(4):
                nat[part, v, rows(rg), :] = vs[v]
            nat[part, 4, rows(rg), :] = corner[part, rows(rg), :]

    def both(value, zl):
        other = turn(value, 64)
        return (jnp.where(low, value, other) if zl == 0 else jnp.where(low, other, value)).astype(
            jnp.int32
        ) + shift

    natv[...] = jnp.zeros_like(natv)
    for mine in range(2):
        parity = core if mine else 1 - core
        for rg in range(4):
            two = [below[8 + yq, rows(rg), :] if mine else vel_other[yq, rows(rg), :] for yq in range(2)]
            vs = swap_blocks(two + two)
            if rg < 3:
                row0, depth = jnp.where(half == 0, 0, 8) + rg * 8, parity
            else:
                row0, depth = jnp.where(half == 0, 0, 24), 2 + parity
            for v in range(4):
                natv[depth, v, pl.ds(pl.multiple_of(row0, 8), 8), :] = (
                    vs[v].astype(jnp.int32) + shift
                )
            value = corner[2, rows(rg), :] if mine else vel_other[4, rows(rg), :]
            for zl in range(2):
                natv[2 * zl + parity, 4, rows(rg), :] = both(value, zl)

    for t in range(4):
        for rg in range(4):
            dst = tile_group(t, rg)
            src = pl.ds((t % 2) * 32 + rg * 8, 8)

            def placed(value):
                return value if t < 2 else turn(value, 32)

            for part in range(2):
                side[part, dst, :] = placed(beside[part, src, :])
            for mine in range(2):
                parity = core if mine else 1 - core
                value = placed(beside[2, src, :] if mine else vel_other[2 + t % 2, rows(rg), :])
                for zl in range(2):
                    sidev[2 * zl + parity, dst, :] = both(value, zl)

    for part in range(2):
        for i in range(OWN):
            for v in range(4):
                term[0, part, i, v] = start[part, i, v]
            term[0, part, i, 4] = side[part, block(i), :]
        for j in range(BLK - OWN):
            for v in range(WAYS):
                term[0, part, OWN + j, v] = nat[part, v, pl.ds(j, 8, stride=4), :]

    def across(x):
        right = jnp.where(last, x[4], turn(x[0], 127))
        left = jnp.where(first, 0.0, turn(x[3], 1))
        back = jnp.where(last, x[3], turn(x[4], 127))
        q = [x[0] + x[1], x[1] + x[2], x[2] + x[3]]
        return [
            (left + x[0]) + q[0],
            q[0] + q[1],
            q[1] + q[2],
            q[2] + (x[3] + right),
            (back + x[4]) + (x[4] + turn(x[4], 1)),
        ]

    def apply(part, source, finish):
        def row(i):
            return across([term[source, part, i, v] for v in range(WAYS)])

        down = {i: [pltpu.roll(h, 1, 0) for h in row(i)] for i in (OWN - 1, BLK - 1)}
        h_own, h_halo = row(0), row(OWN)
        up = {0: [pltpu.roll(h, 7, 0) for h in h_own], OWN: [pltpu.roll(h, 7, 0) for h in h_halo]}

        def ends(at, other, flag, same):
            return [
                jnp.where(sub == at, flag * a, b) for a, b in zip(other, same)
            ]

        chains = (
            (
                range(OWN),
                h_own,
                ends(0, down[BLK - 1], before, down[OWN - 1]),
                ends(7, up[OWN], after, up[0]),
            ),
            (
                range(OWN, BLK),
                h_halo,
                ends(0, down[OWN - 1], after, down[BLK - 1]),
                ends(7, up[0], before, up[OWN]),
            ),
        )
        for span, h_cur, h_low, h_high in chains:
            pair = [a + b for a, b in zip(h_low, h_cur)]
            for i in span:
                h_next = row(i + 1) if i < span[-1] else h_high
                pair_next = [a + b for a, b in zip(h_cur, h_next)]
                for v in range(WAYS):
                    finish(i, v, pair[v] + pair_next[v])
                pair, h_cur = pair_next, h_next

    def combine(i, v, coef):
        real = imag = None
        for k in range(TOP + 1):
            c_re, c_im = coef(2 * k), coef(2 * k + 1)
            t_re = term[k, 0, i, v]
            t_im = term[k, 1, i, v]
            re = c_re * t_re - c_im * t_im
            im = c_re * t_im + c_im * t_re
            real = re if real is None else real + re
            imag = im if imag is None else imag + im
        term[0, 0, i, v] = real
        term[0, 1, i, v] = imag
        return real

    @pl.loop(0, DEPTHS)
    def _(depth):
        for part in range(2):

            def first_term(i, v, s):
                term[1, part, i, v] = 0.125 * s - term[0, part, i, v]

            apply(part, 0, first_term)

        @pl.loop(1, TOP)
        def _(k):
            for part in range(2):

                def next_term(i, v, s):
                    cur = term[k, part, i, v]
                    term[k + 1, part, i, v] = (0.25 * s - cur) - (cur + term[k - 1, part, i, v])

                apply(part, k, next_term)

        @pl.when(depth < AHEAD)
        def _():
            @pl.loop(0, OWN, unroll=16)
            def _(i):
                for v in range(4):
                    img[v, pl.ds(i, 8, stride=PITCH), :] = combine(
                        i, v, lambda n: coefs[depth, i, v, n]
                    )

        @pl.when(depth >= AHEAD)
        def _():
            @pl.loop(0, OWN, unroll=8)
            def _(i):
                for v in range(4):
                    idx = index[depth - AHEAD, i, v]
                    img[v, pl.ds(i, 8, stride=PITCH), :] = combine(
                        i, v, lambda n: gather_lanes(table[n], idx)
                    )

        @pl.when(depth < DEPTHS - 1)
        def _():
            for j in range(BLK - OWN):
                for v in range(WAYS):
                    idx = natv[depth, v, pl.ds(j, 8, stride=4), :]
                    combine(OWN + j, v, lambda n: gather_lanes(table[n], idx))
            for i in range(OWN):
                idx = sidev[depth, block(i), :]
                combine(i, 4, lambda n: gather_lanes(table[n], idx))

        slot = jnp.where(depth % 2 == core, 0, 1)
        zl = depth // 2

        @pl.loop(0, 4, unroll=4)
        def _(n):
            t = own_tile(half, n)
            even = (lane // 32) % 2 == 0
            for rg in range(4):
                vals = [img[v, tile_group(t, rg), :] for v in range(4)]
                vals = [a + turn(a, 64) for a in vals]
                a, b = [jnp.where(low, vals[i], vals[i + 2]) for i in range(2)]
                out[slot, (n * 2 + zl) * 2, rows(rg), :] = jnp.where(even, a, turn(b, 32))
                out[slot, (n * 2 + zl) * 2 + 1, rows(rg), :] = jnp.where(even, turn(a, 96), b)


def extrapolate(*operands):
    vmem = pl.BlockSpec(memory_space=pltpu.VMEM)
    return pl.pallas_call(
        kernel,
        out_shape=jax.ShapeDtypeStruct((2, 16, 32, 128), jnp.float32),
        in_specs=[vmem] * 8,
        out_specs=vmem,
        scratch_shapes=[
            pltpu.VMEM((2, WAYS, 32, 128), jnp.float32),
            pltpu.VMEM((DEPTHS, WAYS, 32, 128), jnp.int32),
            pltpu.VMEM((2, 8 * PITCH, 128), jnp.float32),
            pltpu.VMEM((DEPTHS, 8 * PITCH, 128), jnp.int32),
            pltpu.VMEM((TOP + 1, 2, BLK, WAYS, 8, 128), jnp.float32),
            pltpu.VMEM((4, 8 * PITCH, 128), jnp.float32),
        ],
        compiler_params=pltpu.CompilerParams(vmem_limit_bytes=28 * 1024 * 1024),
        cost_estimate=pl.CostEstimate(flops=70_000_000, bytes_accessed=4_000_000, transcendentals=0),
    )(*operands)


def per_device(surface, coef_table, vel_index):
    groups = groups_of_quadrant()

    with jax.named_scope("pack"):
        send = pack(surface, vel_index)
    with jax.named_scope("tables"):
        x, y, zh, zl, core = coordinates()
        xq = jnp.where(x < 2, x, 3 - x)
        yq = jnp.where(y < 2, y, 3 - y)
        freq = core * 32 + (((xq * 2 + zh) * 2 + zl) * 2 + yq) * 2
        own = lax.dynamic_slice(coef_table, (freq, 0, 0, 0), (2, TOP + 1, 2, NV))
    with jax.named_scope("spread"):
        recv = lax.all_to_all(send, AXES, 0, 0, axis_index_groups=groups)
    with jax.named_scope("halo"):
        below, beside, corner, table = edges(recv, own)
        below = lax.ppermute(below, AXES, pairs(lambda x, y, *rest: (3 - x, y, *rest)))
        beside = lax.ppermute(beside, AXES, pairs(lambda x, y, *rest: (x, 3 - y, *rest)))
        corner = lax.ppermute(corner, AXES, pairs(lambda x, y, *rest: (3 - x, 3 - y, *rest)))
    with jax.named_scope("velocity"):
        vel_other = lax.ppermute(recv[:, 2], AXES, core_pairs())
    with jax.named_scope("prepare"):
        start, index, coefs, zero = prepare(recv, vel_other, table)
    with jax.named_scope("velocity"):
        edge_vel = lax.ppermute(edge_velocity(below, beside, corner, zero), AXES, core_pairs())
    with jax.named_scope("extrapolate"):
        out = extrapolate(start, index, coefs, below, beside, corner, edge_vel, table)
    with jax.named_scope("image"):
        total = out[0] + lax.ppermute(out[1], AXES, core_pairs())
        parts = lax.all_to_all(total, AXES, 0, 0, axis_index_groups=groups)
        return add_up(parts)


def solution(mesh):
    in_specs = (P(None, None, "gx", "gy"), P(), P("sec", "gx", "gy"))
    out_specs = P("sec", "gx", "gy")
    return jax.shard_map(
        per_device, mesh=mesh, in_specs=in_specs, out_specs=out_specs, check_vma=False
    )
```

```python
import jax
import jax.numpy as jnp
from jax import lax
from jax.experimental import pallas as pl
from jax.experimental.pallas import tpu as pltpu
from jax.sharding import PartitionSpec as P

AXES = ("sec", "gx", "gy")
OWN = 16
BLK = 20
PITCH = 24
WAYS = 5
AHEAD = 3
TOP = 8
DEPTHS = 4
NV = 64
COEFS = 2 * (TOP + 1)


def flat(x, y, zh, zl, core):
    return ((zl * 2 + core) * 8 + x * 2 + zh) * 4 + y


def from_rim(half, q):
    return q if half == 0 else 3 - q


def groups_of_quadrant():
    return [
        [
            flat(from_rim(half_x, xq), from_rim(half_y, yq), zh, zl, core)
            for xq in range(2)
            for zh in range(2)
            for zl in range(2)
            for yq in range(2)
        ]
        for half_x in range(2)
        for half_y in range(2)
        for core in range(2)
    ]


def pairs(partner):
    return [
        (flat(x, y, zh, zl, core), flat(*partner(x, y, zh, zl, core)))
        for x in range(4)
        for y in range(4)
        for zh in range(2)
        for zl in range(2)
        for core in range(2)
    ]


def core_pairs():
    return pairs(lambda x, y, zh, zl, core: (x, y, zh, zl, 1 - core))


def gather_lanes(x, idx):
    return jnp.take_along_axis(x, idx, axis=1, mode="promise_in_bounds")


def lanes():
    return lax.broadcasted_iota(jnp.int32, (8, 128), 1)


def rows(rg):
    return pl.ds(rg * 8, 8)


def turn(x, by):
    return pltpu.roll(x, by, 1)


def swap_blocks(x):
    lane = lanes()
    low = lane < 64
    even = (lane // 32) % 2 == 0
    near = [jnp.where(low, x[i], turn(x[i + 2], 64)) for i in range(2)]
    far = [jnp.where(low, turn(x[i], 64), x[i + 2]) for i in range(2)]
    res = []
    for a, b in (near, far):
        res.append(jnp.where(even, a, turn(b, 32)))
        res.append(jnp.where(even, turn(a, 96), b))
    return res


def coordinates():
    sec, gx, y = lax.axis_index("sec"), lax.axis_index("gx"), lax.axis_index("gy")
    x, zh = gx // 2, gx % 2
    return x, y, zh, sec // 2, sec % 2


def pack_kernel(surface, vel, send, buf, vel_buf, sems):
    _, y, _, zl, core = coordinates()
    lane = lanes()
    idx = 4 * (lane % 32) + lane // 32
    idx = jnp.where(y < 2, idx, 127 - idx)
    vel_copy = pltpu.make_async_copy(vel, vel_buf, sems.at[4])
    vel_copy.start()
    copies = [
        pltpu.make_async_copy(
            surface.at[pl.ds(core * 16 + j * 4, 4), zl], buf.at[pl.ds(j * 4, 4)], sems.at[j]
        )
        for j in range(4)
    ]
    for copy in copies:
        copy.start()
    vel_copy.wait()
    for rg in range(4):
        value = gather_lanes(vel_buf[0, rows(rg), :].astype(jnp.float32), idx)
        for n in range(16):
            send[n, 2, rows(rg), :] = value
    for j, copy in enumerate(copies):
        copy.wait()
        for n in range(j * 4, j * 4 + 4):
            for part in range(2):
                for rg in range(4):
                    send[n, part, rows(rg), :] = gather_lanes(buf[n, part, rows(rg), :], idx)


def pack(surface, vel):
    vmem = pl.BlockSpec(memory_space=pltpu.VMEM)
    return pl.pallas_call(
        pack_kernel,
        out_shape=jax.ShapeDtypeStruct((16, 3, 32, 128), jnp.float32),
        in_specs=[pl.BlockSpec(memory_space=pl.ANY)] * 2,
        out_specs=vmem,
        scratch_shapes=[
            pltpu.VMEM((16, 2, 32, 128), jnp.float32),
            pltpu.VMEM((1, 32, 128), jnp.int32),
            pltpu.SemaphoreType.DMA((5,)),
        ],
        compiler_params=pltpu.CompilerParams(vmem_limit_bytes=60 * 1024 * 1024),
    )(surface.reshape(32, 2, 2, 32, 128), vel)


def sum_kernel(parts, image):
    y = lax.axis_index("gy")
    lane = lanes()
    column = jnp.where(y < 2, lane, 127 - lane)
    idx = 32 * (column % 4) + column // 4
    for rg in range(4):
        terms = [parts[n, rows(rg), :] for n in range(16)]
        while len(terms) > 1:
            terms = [a + b for a, b in zip(terms[::2], terms[1::2])]
        image[0, rows(rg), :] = gather_lanes(terms[0], idx)


def add_up(parts):
    vmem = pl.BlockSpec(memory_space=pltpu.VMEM)
    return pl.pallas_call(
        sum_kernel,
        out_shape=jax.ShapeDtypeStruct((1, 32, 128), jnp.float32),
        in_specs=[vmem],
        out_specs=vmem,
        compiler_params=pltpu.CompilerParams(vmem_limit_bytes=16 * 1024 * 1024),
    )(parts)


def own_tile(half, n):
    return jnp.where(half == 0, n, (n + 2) % 4)


def edge_kernel(recv, own, below, beside, corner, table):
    x, _, _, _, _ = coordinates()
    half = x // 2
    lane = lanes()
    inner = lane % 32
    block = lane // 32
    last = 32 * (inner % 4) + 24 + inner // 4
    edge = 2 + (1 - half)
    for k in range(TOP + 1):
        pair = jnp.concatenate([own[0, k], own[1, k]], axis=1)
        for r in range(2):
            table[2 * k + r] = jnp.broadcast_to(pair[r : r + 1], (8, 128))

    for yq in range(2):
        for rg in range(4):
            for f in range(2):
                for part in range(2):
                    below[(f * 2 + part) * 2 + yq, rows(rg), :] = recv[
                        (edge * 2 + f) * 2 + yq, part, rows(rg), :
                    ]
            if rg < 3:
                zl, row0 = 0, 8 * (1 - half) + rg * 8
            else:
                zl, row0 = 1, 24 * (1 - half)
            below[8 + yq, rows(rg), :] = recv[
                (edge * 2 + zl) * 2 + yq, 2, pl.ds(pl.multiple_of(row0, 8), 8), :
            ]

    def final_columns(n, f, slab, rg):
        return gather_lanes(recv[(n * 2 + f) * 2 + 1, slab, rows(rg), :], last)

    for rg in range(4):
        for slab in range(3):
            a, b = [final_columns(edge, f, slab, rg) for f in range(2)]
            corner[slab, rows(rg), :] = jnp.where(lane < 64, a, b)
            for t in range(2):
                near, far = own_tile(half, t), own_tile(half, t + 2)
                a, b, c, d = [
                    final_columns(n, f, slab, rg) for f in range(2) for n in (far, near)
                ]
                beside[slab, pl.ds(t * 32 + rg * 8, 8), :] = jnp.where(
                    block < 2, jnp.where(block == 0, a, b), jnp.where(block == 2, c, d)
                )


def edges(recv, own):
    vmem = pl.BlockSpec(memory_space=pltpu.VMEM)
    return pl.pallas_call(
        edge_kernel,
        out_shape=(
            jax.ShapeDtypeStruct((10, 32, 128), jnp.float32),
            jax.ShapeDtypeStruct((3, 64, 128), jnp.float32),
            jax.ShapeDtypeStruct((3, 32, 128), jnp.float32),
            jax.ShapeDtypeStruct((COEFS, 8, 128), jnp.float32),
        ),
        in_specs=[vmem] * 2,
        out_specs=(vmem,) * 4,
        compiler_params=pltpu.CompilerParams(vmem_limit_bytes=16 * 1024 * 1024),
    )(recv, own)


def edge_velocity_kernel(below, beside, corner, zero, vel):
    for rg in range(4):
        for q in range(2):
            vel[q, rows(rg), :] = below[8 + q, rows(rg), :] + zero[...]
            vel[2 + q, rows(rg), :] = beside[2, pl.ds(q * 32 + rg * 8, 8), :]
        vel[4, rows(rg), :] = corner[2, rows(rg), :]


def edge_velocity(*operands):
    vmem = pl.BlockSpec(memory_space=pltpu.VMEM)
    return pl.pallas_call(
        edge_velocity_kernel,
        out_shape=jax.ShapeDtypeStruct((5, 32, 128), jnp.float32),
        in_specs=[vmem] * 4,
        out_specs=vmem,
        compiler_params=pltpu.CompilerParams(vmem_limit_bytes=16 * 1024 * 1024),
    )(*operands)


def tile_group(t, rg):
    return pl.ds(pl.multiple_of((2 * t + rg // 2) * PITCH + 8 * (rg % 2), 8), 8)


def prepare_kernel(recv, vel_other, table, start, index, coefs, zero, nat, natv):
    x, _, _, _, core = coordinates()
    zero[...] = jnp.zeros_like(zero)
    half = x // 2
    shift = jnp.where(lanes() < 64, 0, NV)

    @pl.loop(0, 4)
    def _(n):
        t = own_tile(half, n)
        for rg in range(4):
            dst = tile_group(t, rg)
            for part in range(2):
                vs = swap_blocks([recv[n * 4 + m, part, rows(rg), :] for m in range(4)])
                for v in range(4):
                    nat[part, v, dst, :] = vs[v]
            for zl in range(2):
                for mine in range(2):
                    two = [
                        recv[n * 4 + zl * 2 + yq, 2, rows(rg), :]
                        if mine
                        else vel_other[n * 4 + zl * 2 + yq, rows(rg), :]
                        for yq in range(2)
                    ]
                    depth = zl * 2 + (core if mine else 1 - core)
                    vs = swap_blocks(two + two)
                    for v in range(4):
                        natv[depth, v, dst, :] = vs[v].astype(jnp.int32) + shift

    def block(i):
        return pl.ds(i, 8, stride=PITCH)

    for i in range(OWN):
        for v in range(4):
            for part in range(2):
                start[part, i, v] = nat[part, v, block(i), :]
            for depth in range(AHEAD, DEPTHS):
                index[depth - AHEAD, i, v] = natv[depth, v, block(i), :]

    @pl.loop(0, AHEAD)
    def _(depth):
        @pl.loop(0, OWN, unroll=16)
        def _(i):
            for v in range(4):
                idx = natv[depth, v, block(i), :]
                for n in range(COEFS):
                    coefs[depth, i, v, n] = gather_lanes(table[n], idx)


def prepare(recv, vel_other, table):
    vmem = pl.BlockSpec(memory_space=pltpu.VMEM)
    return pl.pallas_call(
        prepare_kernel,
        out_shape=(
            jax.ShapeDtypeStruct((2, OWN, 4, 8, 128), jnp.float32),
            jax.ShapeDtypeStruct((DEPTHS - AHEAD, OWN, 4, 8, 128), jnp.int32),
            jax.ShapeDtypeStruct((AHEAD, OWN, 4, COEFS, 8, 128), jnp.float32),
            jax.ShapeDtypeStruct((8, 128), jnp.float32),
        ),
        in_specs=[vmem] * 3,
        out_specs=(vmem,) * 4,
        scratch_shapes=[
            pltpu.VMEM((2, 4, 8 * PITCH, 128), jnp.float32),
            pltpu.VMEM((DEPTHS, 4, 8 * PITCH, 128), jnp.int32),
        ],
        compiler_params=pltpu.CompilerParams(vmem_limit_bytes=8 * 1024 * 1024),
        cost_estimate=pl.CostEstimate(flops=20_000_000, bytes_accessed=4_000_000, transcendentals=0),
    )(recv, vel_other, table)


def late_kernel(index, table, coefs):
    for depth in range(DEPTHS - AHEAD):

        @pl.loop(0, OWN, unroll=16)
        def _(i):
            for v in range(4):
                idx = index[depth, i, v]
                for n in range(COEFS):
                    coefs[depth, i, v, n] = gather_lanes(table[n], idx)


def late(index, table):
    vmem = pl.BlockSpec(memory_space=pltpu.VMEM)
    return pl.pallas_call(
        late_kernel,
        out_shape=jax.ShapeDtypeStruct((DEPTHS - AHEAD, OWN, 4, COEFS, 8, 128), jnp.float32),
        in_specs=[vmem] * 2,
        out_specs=vmem,
        compiler_params=pltpu.CompilerParams(vmem_limit_bytes=8 * 1024 * 1024),
        cost_estimate=pl.CostEstimate(flops=5_000_000, bytes_accessed=1_000_000, transcendentals=0),
    )(index, table)


def kernel(
    start, late_coefs, coefs, below, beside, corner, vel_other, table, out,
    nat, natv, side, sidev, term, pair_sum, img
):
    x, _, _, _, core = coordinates()
    half = x // 2
    lane = lanes()
    sub = lax.broadcasted_iota(jnp.int32, (8, 128), 0)
    first = lane % 64 == 0
    last = lane % 64 == 63
    low = lane < 64
    shift = jnp.where(low, 0, NV)
    rim = {0: (sub == 0) & (half == 0), 7: (sub == 7) & (half == 1)}

    def block(i):
        return pl.ds(i, 8, stride=PITCH)

    for part in range(2):
        for rg in range(4):
            vs = swap_blocks(
                [below[(f * 2 + part) * 2 + yq, rows(rg), :] for f in range(2) for yq in range(2)]
            )
            for v in range(4):
                nat[part, v, rows(rg), :] = vs[v]
            nat[part, 4, rows(rg), :] = corner[part, rows(rg), :]

    def both(value, zl):
        other = turn(value, 64)
        return (jnp.where(low, value, other) if zl == 0 else jnp.where(low, other, value)).astype(
            jnp.int32
        ) + shift

    natv[...] = jnp.zeros_like(natv)
    for mine in range(2):
        parity = core if mine else 1 - core
        for rg in range(4):
            two = [below[8 + yq, rows(rg), :] if mine else vel_other[yq, rows(rg), :] for yq in range(2)]
            vs = swap_blocks(two + two)
            if rg < 3:
                row0, depth = jnp.where(half == 0, 0, 8) + rg * 8, parity
            else:
                row0, depth = jnp.where(half == 0, 0, 24), 2 + parity
            for v in range(4):
                natv[depth, v, pl.ds(pl.multiple_of(row0, 8), 8), :] = (
                    vs[v].astype(jnp.int32) + shift
                )
            value = corner[2, rows(rg), :] if mine else vel_other[4, rows(rg), :]
            for zl in range(2):
                natv[2 * zl + parity, 4, rows(rg), :] = both(value, zl)

    for t in range(4):
        for rg in range(4):
            dst = tile_group(t, rg)
            src = pl.ds((t % 2) * 32 + rg * 8, 8)

            def placed(value):
                return value if t < 2 else turn(value, 32)

            for part in range(2):
                side[part, dst, :] = placed(beside[part, src, :])
            for mine in range(2):
                parity = core if mine else 1 - core
                value = placed(beside[2, src, :] if mine else vel_other[2 + t % 2, rows(rg), :])
                for zl in range(2):
                    sidev[2 * zl + parity, dst, :] = both(value, zl)

    for part in range(2):
        for i in range(OWN):
            for v in range(4):
                term[0, part, i, v] = start[part, i, v]
            term[0, part, i, 4] = side[part, block(i), :]
        for j in range(BLK - OWN):
            for v in range(WAYS):
                term[0, part, OWN + j, v] = nat[part, v, pl.ds(j, 8, stride=4), :]

    def across(x):
        right = jnp.where(last, x[4], turn(x[0], 127))
        left = jnp.where(first, 0.0, turn(x[3], 1))
        back = jnp.where(last, x[3], turn(x[4], 127))
        q = [x[0] + x[1], x[1] + x[2], x[2] + x[3]]
        return [
            (left + x[0]) + q[0],
            q[0] + q[1],
            q[1] + q[2],
            q[2] + (x[3] + right),
            (back + x[4]) + (x[4] + turn(x[4], 1)),
        ]

    def apply(part, source, finish):
        def row(i):
            return across([term[source, part, i, v] for v in range(WAYS)])

        known = {i: row(i) for i in (0, OWN - 1, OWN, BLK - 1)}
        down = {i: [pltpu.roll(h, 1, 0) for h in known[i]] for i in (OWN - 1, BLK - 1)}
        up = {i: [pltpu.roll(h, 7, 0) for h in known[i]] for i in (0, OWN)}

        def ends(at, other, same):
            return [jnp.where(sub == at, a, b) for a, b in zip(other, same)]

        def open_ends(at, other, same):
            return [jnp.where(rim[at], 0.0, a) for a in ends(at, other, same)]

        chains = (
            (
                range(OWN),
                known[0],
                open_ends(0, down[BLK - 1], down[OWN - 1]),
                open_ends(7, up[OWN], up[0]),
            ),
            (
                range(OWN, BLK),
                known[OWN],
                ends(0, down[OWN - 1], down[BLK - 1]),
                ends(7, up[0], up[OWN]),
            ),
        )
        for span, h_cur, h_low, h_high in chains:
            pair = [a + b for a, b in zip(h_low, h_cur)]
            for i in span:
                if i == span[-1]:
                    h_next = h_high
                else:
                    h_next = known[i + 1] if i + 1 in known else row(i + 1)
                pair_next = [a + b for a, b in zip(h_cur, h_next)]
                for v in range(WAYS):
                    finish(i, v, pair[v] + pair_next[v])
                pair, h_cur = pair_next, h_next

    def combine(i, v, coef):
        real = imag = None
        for k in range(TOP + 1):
            c_re, c_im = coef(2 * k), coef(2 * k + 1)
            t_re = term[k, 0, i, v]
            t_im = term[k, 1, i, v]
            re = c_re * t_re - c_im * t_im
            im = c_re * t_im + c_im * t_re
            real = re if real is None else real + re
            imag = im if imag is None else imag + im
        term[0, 0, i, v] = real
        term[0, 1, i, v] = imag
        return real

    @pl.loop(0, DEPTHS)
    def _(depth):
        for part in range(2):

            def first_term(i, v, s):
                new = 0.125 * s
                pair_sum[part, i, v] = new
                term[1, part, i, v] = new - term[0, part, i, v]

            apply(part, 0, first_term)

        @pl.loop(1, TOP, unroll=TOP - 1)
        def _(k):
            for part in range(2):

                def next_term(i, v, s):
                    new = 0.25 * s - pair_sum[part, i, v]
                    pair_sum[part, i, v] = new
                    term[k + 1, part, i, v] = new - term[k, part, i, v]

                apply(part, k, next_term)

        def combine_own(ref, step):
            @pl.loop(0, OWN, unroll=16)
            def _(i):
                for v in range(4):
                    img[v, pl.ds(i, 8, stride=PITCH), :] = combine(
                        i, v, lambda n: ref[step, i, v, n]
                    )

        @pl.when(depth < AHEAD)
        def _():
            combine_own(coefs, depth)

        @pl.when(depth >= AHEAD)
        def _():
            combine_own(late_coefs, depth - AHEAD)

        @pl.when(depth < DEPTHS - 1)
        def _():
            for j in range(BLK - OWN):
                for v in range(WAYS):
                    idx = natv[depth, v, pl.ds(j, 8, stride=4), :]
                    combine(OWN + j, v, lambda n: gather_lanes(table[n], idx))
            for i in range(OWN):
                idx = sidev[depth, block(i), :]
                combine(i, 4, lambda n: gather_lanes(table[n], idx))

        slot = jnp.where(depth % 2 == core, 0, 1)
        zl = depth // 2

        @pl.loop(0, 4, unroll=4)
        def _(n):
            t = own_tile(half, n)
            even = (lane // 32) % 2 == 0
            for rg in range(4):
                vals = [img[v, tile_group(t, rg), :] for v in range(4)]
                vals = [a + turn(a, 64) for a in vals]
                a, b = [jnp.where(low, vals[i], vals[i + 2]) for i in range(2)]
                out[slot, (n * 2 + zl) * 2, rows(rg), :] = jnp.where(even, a, turn(b, 32))
                out[slot, (n * 2 + zl) * 2 + 1, rows(rg), :] = jnp.where(even, turn(a, 96), b)


def extrapolate(*operands):
    vmem = pl.BlockSpec(memory_space=pltpu.VMEM)
    return pl.pallas_call(
        kernel,
        out_shape=jax.ShapeDtypeStruct((2, 16, 32, 128), jnp.float32),
        in_specs=[vmem] * 8,
        out_specs=vmem,
        scratch_shapes=[
            pltpu.VMEM((2, WAYS, 32, 128), jnp.float32),
            pltpu.VMEM((DEPTHS, WAYS, 32, 128), jnp.int32),
            pltpu.VMEM((2, 8 * PITCH, 128), jnp.float32),
            pltpu.VMEM((DEPTHS, 8 * PITCH, 128), jnp.int32),
            pltpu.VMEM((TOP + 1, 2, BLK, WAYS, 8, 128), jnp.float32),
            pltpu.VMEM((2, BLK, WAYS, 8, 128), jnp.float32),
            pltpu.VMEM((4, 8 * PITCH, 128), jnp.float32),
        ],
        compiler_params=pltpu.CompilerParams(vmem_limit_bytes=14 * 1024 * 1024),
        cost_estimate=pl.CostEstimate(flops=70_000_000, bytes_accessed=4_000_000, transcendentals=0),
    )(*operands)


def per_device(surface, coef_table, vel_index):
    groups = groups_of_quadrant()

    with jax.named_scope("pack"):
        send = pack(surface, vel_index)
    with jax.named_scope("tables"):
        x, y, zh, zl, core = coordinates()
        xq = jnp.where(x < 2, x, 3 - x)
        yq = jnp.where(y < 2, y, 3 - y)
        freq = core * 32 + (((xq * 2 + zh) * 2 + zl) * 2 + yq) * 2
        own = lax.dynamic_slice(coef_table, (freq, 0, 0, 0), (2, TOP + 1, 2, NV))
    with jax.named_scope("spread"):
        recv = lax.all_to_all(send, AXES, 0, 0, axis_index_groups=groups)
    with jax.named_scope("halo"):
        below, beside, corner, table = edges(recv, own)
        below = lax.ppermute(below, AXES, pairs(lambda x, y, *rest: (3 - x, y, *rest)))
        beside = lax.ppermute(beside, AXES, pairs(lambda x, y, *rest: (x, 3 - y, *rest)))
        corner = lax.ppermute(corner, AXES, pairs(lambda x, y, *rest: (3 - x, 3 - y, *rest)))
    with jax.named_scope("velocity"):
        vel_other = lax.ppermute(recv[:, 2], AXES, core_pairs())
    with jax.named_scope("prepare"):
        start, index, coefs, zero = prepare(recv, vel_other, table)
    with jax.named_scope("velocity"):
        edge_vel = lax.ppermute(edge_velocity(below, beside, corner, zero), AXES, core_pairs())
    with jax.named_scope("late"):
        late_coefs = late(index, table)
    with jax.named_scope("extrapolate"):
        out = extrapolate(start, late_coefs, coefs, below, beside, corner, edge_vel, table)
    with jax.named_scope("image"):
        total = out[0] + lax.ppermute(out[1], AXES, core_pairs())
        parts = lax.all_to_all(total, AXES, 0, 0, axis_index_groups=groups)
        return add_up(parts)


def solution(mesh):
    in_specs = (P(None, None, "gx", "gy"), P(), P("sec", "gx", "gy"))
    out_specs = P("sec", "gx", "gy")
    return jax.shard_map(
        per_device, mesh=mesh, in_specs=in_specs, out_specs=out_specs, check_vma=False
    )
```

```python
import jax
import jax.numpy as jnp
from jax import lax
from jax.experimental import pallas as pl
from jax.experimental.pallas import tpu as pltpu
from jax.sharding import PartitionSpec as P

AXES = ("sec", "gx", "gy")
OWN = 16
BLK = 20
PITCH = 24
WAYS = 5
AHEAD = 3
TOP = 8
DEPTHS = 4
NV = 64
COEFS = 2 * (TOP + 1)
BY_ROW = 6


def flat(x, y, zh, zl, core):
    return ((zl * 2 + core) * 8 + x * 2 + zh) * 4 + y


def from_rim(half, q):
    return q if half == 0 else 3 - q


def groups_of_quadrant():
    return [
        [
            flat(from_rim(half_x, xq), from_rim(half_y, yq), zh, zl, core)
            for xq in range(2)
            for zh in range(2)
            for zl in range(2)
            for yq in range(2)
        ]
        for half_x in range(2)
        for half_y in range(2)
        for core in range(2)
    ]


def pairs(partner):
    return [
        (flat(x, y, zh, zl, core), flat(*partner(x, y, zh, zl, core)))
        for x in range(4)
        for y in range(4)
        for zh in range(2)
        for zl in range(2)
        for core in range(2)
    ]


def core_pairs():
    return pairs(lambda x, y, zh, zl, core: (x, y, zh, zl, 1 - core))


def gather_lanes(x, idx):
    return jnp.take_along_axis(x, idx, axis=1, mode="promise_in_bounds")


def gather_rows(x, idx):
    return jnp.take_along_axis(x, idx, axis=0, mode="promise_in_bounds")


def look_up(indices, table, row_table, store):
    low = [idx & 7 for idx in indices]
    bits = [[(idx & (8 << b)) == 0 for b in range(3)] for idx in indices]
    for v, idx in enumerate(indices):
        for n in range(BY_ROW, COEFS):
            store(v, n, gather_lanes(table[n], idx))
    for n in range(BY_ROW):
        entries = [row_table[n, j] for j in range(8)]
        for v in range(len(indices)):
            level = [gather_rows(e, low[v]) for e in entries]
            for bit in bits[v]:
                level = [jnp.where(bit, a, b) for a, b in zip(level[::2], level[1::2])]
            store(v, n, level[0])


def lanes():
    return lax.broadcasted_iota(jnp.int32, (8, 128), 1)


def rows(rg):
    return pl.ds(rg * 8, 8)


def turn(x, by):
    return pltpu.roll(x, by, 1)


def swap_blocks(x):
    lane = lanes()
    low = lane < 64
    even = (lane // 32) % 2 == 0
    near = [jnp.where(low, x[i], turn(x[i + 2], 64)) for i in range(2)]
    far = [jnp.where(low, turn(x[i], 64), x[i + 2]) for i in range(2)]
    res = []
    for a, b in (near, far):
        res.append(jnp.where(even, a, turn(b, 32)))
        res.append(jnp.where(even, turn(a, 96), b))
    return res


def coordinates():
    sec, gx, y = lax.axis_index("sec"), lax.axis_index("gx"), lax.axis_index("gy")
    x, zh = gx // 2, gx % 2
    return x, y, zh, sec // 2, sec % 2


def pack_kernel(surface, vel, send, buf, vel_buf, sems):
    _, y, _, zl, core = coordinates()
    lane = lanes()
    idx = 4 * (lane % 32) + lane // 32
    idx = jnp.where(y < 2, idx, 127 - idx)
    vel_copy = pltpu.make_async_copy(vel, vel_buf, sems.at[4])
    vel_copy.start()
    copies = [
        pltpu.make_async_copy(
            surface.at[pl.ds(core * 16 + j * 4, 4), zl], buf.at[pl.ds(j * 4, 4)], sems.at[j]
        )
        for j in range(4)
    ]
    for copy in copies:
        copy.start()
    vel_copy.wait()
    for rg in range(4):
        value = gather_lanes(vel_buf[0, rows(rg), :].astype(jnp.float32), idx)
        for n in range(16):
            send[n, 2, rows(rg), :] = value
    for j, copy in enumerate(copies):
        copy.wait()
        for n in range(j * 4, j * 4 + 4):
            for part in range(2):
                for rg in range(4):
                    send[n, part, rows(rg), :] = gather_lanes(buf[n, part, rows(rg), :], idx)


def pack(surface, vel):
    vmem = pl.BlockSpec(memory_space=pltpu.VMEM)
    return pl.pallas_call(
        pack_kernel,
        out_shape=jax.ShapeDtypeStruct((16, 3, 32, 128), jnp.float32),
        in_specs=[pl.BlockSpec(memory_space=pl.ANY)] * 2,
        out_specs=vmem,
        scratch_shapes=[
            pltpu.VMEM((16, 2, 32, 128), jnp.float32),
            pltpu.VMEM((1, 32, 128), jnp.int32),
            pltpu.SemaphoreType.DMA((5,)),
        ],
        compiler_params=pltpu.CompilerParams(vmem_limit_bytes=60 * 1024 * 1024),
    )(surface.reshape(32, 2, 2, 32, 128), vel)


def sum_kernel(parts, image):
    y = lax.axis_index("gy")
    lane = lanes()
    column = jnp.where(y < 2, lane, 127 - lane)
    idx = 32 * (column % 4) + column // 4
    for rg in range(4):
        terms = [parts[n, rows(rg), :] for n in range(16)]
        while len(terms) > 1:
            terms = [a + b for a, b in zip(terms[::2], terms[1::2])]
        image[0, rows(rg), :] = gather_lanes(terms[0], idx)


def add_up(parts):
    vmem = pl.BlockSpec(memory_space=pltpu.VMEM)
    return pl.pallas_call(
        sum_kernel,
        out_shape=jax.ShapeDtypeStruct((1, 32, 128), jnp.float32),
        in_specs=[vmem],
        out_specs=vmem,
        compiler_params=pltpu.CompilerParams(vmem_limit_bytes=16 * 1024 * 1024),
    )(parts)


def own_tile(half, n):
    return jnp.where(half == 0, n, (n + 2) % 4)


def edge_kernel(recv, own, below, beside, corner, table):
    x, _, _, _, _ = coordinates()
    half = x // 2
    lane = lanes()
    inner = lane % 32
    block = lane // 32
    last = 32 * (inner % 4) + 24 + inner // 4
    edge = 2 + (1 - half)
    for k in range(TOP + 1):
        pair = jnp.concatenate([own[0, k], own[1, k]], axis=1)
        for r in range(2):
            table[2 * k + r] = jnp.broadcast_to(pair[r : r + 1], (8, 128))

    for yq in range(2):
        for rg in range(4):
            for f in range(2):
                for part in range(2):
                    below[(f * 2 + part) * 2 + yq, rows(rg), :] = recv[
                        (edge * 2 + f) * 2 + yq, part, rows(rg), :
                    ]
            if rg < 3:
                zl, row0 = 0, 8 * (1 - half) + rg * 8
            else:
                zl, row0 = 1, 24 * (1 - half)
            below[8 + yq, rows(rg), :] = recv[
                (edge * 2 + zl) * 2 + yq, 2, pl.ds(pl.multiple_of(row0, 8), 8), :
            ]

    def final_columns(n, f, slab, rg):
        return gather_lanes(recv[(n * 2 + f) * 2 + 1, slab, rows(rg), :], last)

    for rg in range(4):
        for slab in range(3):
            a, b = [final_columns(edge, f, slab, rg) for f in range(2)]
            corner[slab, rows(rg), :] = jnp.where(lane < 64, a, b)
            for t in range(2):
                near, far = own_tile(half, t), own_tile(half, t + 2)
                a, b, c, d = [
                    final_columns(n, f, slab, rg) for f in range(2) for n in (far, near)
                ]
                beside[slab, pl.ds(t * 32 + rg * 8, 8), :] = jnp.where(
                    block < 2, jnp.where(block == 0, a, b), jnp.where(block == 2, c, d)
                )


def edges(recv, own):
    vmem = pl.BlockSpec(memory_space=pltpu.VMEM)
    return pl.pallas_call(
        edge_kernel,
        out_shape=(
            jax.ShapeDtypeStruct((10, 32, 128), jnp.float32),
            jax.ShapeDtypeStruct((3, 64, 128), jnp.float32),
            jax.ShapeDtypeStruct((3, 32, 128), jnp.float32),
            jax.ShapeDtypeStruct((COEFS, 8, 128), jnp.float32),
        ),
        in_specs=[vmem] * 2,
        out_specs=(vmem,) * 4,
        compiler_params=pltpu.CompilerParams(vmem_limit_bytes=16 * 1024 * 1024),
    )(recv, own)


def edge_velocity_kernel(below, beside, corner, zero, vel):
    for rg in range(4):
        for q in range(2):
            vel[q, rows(rg), :] = below[8 + q, rows(rg), :] + zero[...]
            vel[2 + q, rows(rg), :] = beside[2, pl.ds(q * 32 + rg * 8, 8), :]
        vel[4, rows(rg), :] = corner[2, rows(rg), :]


def edge_velocity(*operands):
    vmem = pl.BlockSpec(memory_space=pltpu.VMEM)
    return pl.pallas_call(
        edge_velocity_kernel,
        out_shape=jax.ShapeDtypeStruct((5, 32, 128), jnp.float32),
        in_specs=[vmem] * 4,
        out_specs=vmem,
        compiler_params=pltpu.CompilerParams(vmem_limit_bytes=16 * 1024 * 1024),
    )(*operands)


def tile_group(t, rg):
    return pl.ds(pl.multiple_of((2 * t + rg // 2) * PITCH + 8 * (rg % 2), 8), 8)


def prepare_kernel(
    recv, vel_other, table, start, index, coefs, row_table, zero, nat, natv
):
    x, _, _, _, core = coordinates()
    zero[...] = jnp.zeros_like(zero)
    entry = lax.broadcasted_iota(jnp.int32, (8, 128), 0) + jnp.where(lanes() < 64, 0, NV)
    for j in range(8):
        for n in range(BY_ROW):
            row_table[n, j] = gather_lanes(table[n], entry + 8 * j)
    half = x // 2
    shift = jnp.where(lanes() < 64, 0, NV)

    @pl.loop(0, 4)
    def _(n):
        t = own_tile(half, n)
        for rg in range(4):
            dst = tile_group(t, rg)
            for part in range(2):
                vs = swap_blocks([recv[n * 4 + m, part, rows(rg), :] for m in range(4)])
                for v in range(4):
                    nat[part, v, dst, :] = vs[v]
            for zl in range(2):
                for mine in range(2):
                    two = [
                        recv[n * 4 + zl * 2 + yq, 2, rows(rg), :]
                        if mine
                        else vel_other[n * 4 + zl * 2 + yq, rows(rg), :]
                        for yq in range(2)
                    ]
                    depth = zl * 2 + (core if mine else 1 - core)
                    vs = swap_blocks(two + two)
                    for v in range(4):
                        natv[depth, v, dst, :] = vs[v].astype(jnp.int32) + shift

    def block(i):
        return pl.ds(i, 8, stride=PITCH)

    for i in range(OWN):
        for v in range(4):
            for part in range(2):
                start[part, i, v] = nat[part, v, block(i), :]
            for depth in range(AHEAD, DEPTHS):
                index[depth - AHEAD, i, v] = natv[depth, v, block(i), :]

    @pl.loop(0, AHEAD)
    def _(depth):
        @pl.loop(0, OWN, unroll=16)
        def _(i):
            def store(v, n, value):
                coefs[depth, i, v, n] = value

            look_up([natv[depth, v, block(i), :] for v in range(4)], table, row_table, store)


def prepare(recv, vel_other, table):
    vmem = pl.BlockSpec(memory_space=pltpu.VMEM)
    return pl.pallas_call(
        prepare_kernel,
        out_shape=(
            jax.ShapeDtypeStruct((2, OWN, 4, 8, 128), jnp.float32),
            jax.ShapeDtypeStruct((DEPTHS - AHEAD, OWN, 4, 8, 128), jnp.int32),
            jax.ShapeDtypeStruct((AHEAD, OWN, 4, COEFS, 8, 128), jnp.float32),
            jax.ShapeDtypeStruct((BY_ROW, 8, 8, 128), jnp.float32),
            jax.ShapeDtypeStruct((8, 128), jnp.float32),
        ),
        in_specs=[vmem] * 3,
        out_specs=(vmem,) * 5,
        scratch_shapes=[
            pltpu.VMEM((2, 4, 8 * PITCH, 128), jnp.float32),
            pltpu.VMEM((DEPTHS, 4, 8 * PITCH, 128), jnp.int32),
        ],
        compiler_params=pltpu.CompilerParams(vmem_limit_bytes=8 * 1024 * 1024),
        cost_estimate=pl.CostEstimate(flops=20_000_000, bytes_accessed=4_000_000, transcendentals=0),
    )(recv, vel_other, table)


def late_kernel(index, table, row_table, coefs):
    for depth in range(DEPTHS - AHEAD):

        @pl.loop(0, OWN, unroll=16)
        def _(i):
            def store(v, n, value):
                coefs[depth, i, v, n] = value

            look_up([index[depth, i, v] for v in range(4)], table, row_table, store)


def late(index, table, row_table):
    vmem = pl.BlockSpec(memory_space=pltpu.VMEM)
    return pl.pallas_call(
        late_kernel,
        out_shape=jax.ShapeDtypeStruct((DEPTHS - AHEAD, OWN, 4, COEFS, 8, 128), jnp.float32),
        in_specs=[vmem] * 3,
        out_specs=vmem,
        compiler_params=pltpu.CompilerParams(vmem_limit_bytes=8 * 1024 * 1024),
        cost_estimate=pl.CostEstimate(flops=5_000_000, bytes_accessed=1_000_000, transcendentals=0),
    )(index, table, row_table)


def kernel(
    start, late_coefs, coefs, below, beside, corner, vel_other, table, out,
    nat, natv, side, sidev, term, pair_sum, img
):
    x, _, _, _, core = coordinates()
    half = x // 2
    lane = lanes()
    sub = lax.broadcasted_iota(jnp.int32, (8, 128), 0)
    first = lane % 64 == 0
    last = lane % 64 == 63
    low = lane < 64
    shift = jnp.where(low, 0, NV)
    rim = {0: (sub == 0) & (half == 0), 7: (sub == 7) & (half == 1)}

    def block(i):
        return pl.ds(i, 8, stride=PITCH)

    for part in range(2):
        for rg in range(4):
            vs = swap_blocks(
                [below[(f * 2 + part) * 2 + yq, rows(rg), :] for f in range(2) for yq in range(2)]
            )
            for v in range(4):
                nat[part, v, rows(rg), :] = vs[v]
            nat[part, 4, rows(rg), :] = corner[part, rows(rg), :]

    def both(value, zl):
        other = turn(value, 64)
        return (jnp.where(low, value, other) if zl == 0 else jnp.where(low, other, value)).astype(
            jnp.int32
        ) + shift

    natv[...] = jnp.zeros_like(natv)
    for mine in range(2):
        parity = core if mine else 1 - core
        for rg in range(4):
            two = [below[8 + yq, rows(rg), :] if mine else vel_other[yq, rows(rg), :] for yq in range(2)]
            vs = swap_blocks(two + two)
            if rg < 3:
                row0, depth = jnp.where(half == 0, 0, 8) + rg * 8, parity
            else:
                row0, depth = jnp.where(half == 0, 0, 24), 2 + parity
            for v in range(4):
                natv[depth, v, pl.ds(pl.multiple_of(row0, 8), 8), :] = (
                    vs[v].astype(jnp.int32) + shift
                )
            value = corner[2, rows(rg), :] if mine else vel_other[4, rows(rg), :]
            for zl in range(2):
                natv[2 * zl + parity, 4, rows(rg), :] = both(value, zl)

    for t in range(4):
        for rg in range(4):
            dst = tile_group(t, rg)
            src = pl.ds((t % 2) * 32 + rg * 8, 8)

            def placed(value):
                return value if t < 2 else turn(value, 32)

            for part in range(2):
                side[part, dst, :] = placed(beside[part, src, :])
            for mine in range(2):
                parity = core if mine else 1 - core
                value = placed(beside[2, src, :] if mine else vel_other[2 + t % 2, rows(rg), :])
                for zl in range(2):
                    sidev[2 * zl + parity, dst, :] = both(value, zl)

    for part in range(2):
        for i in range(OWN):
            for v in range(4):
                term[0, part, i, v] = start[part, i, v]
            term[0, part, i, 4] = side[part, block(i), :]
        for j in range(BLK - OWN):
            for v in range(WAYS):
                term[0, part, OWN + j, v] = nat[part, v, pl.ds(j, 8, stride=4), :]

    def across(x):
        right = jnp.where(last, x[4], turn(x[0], 127))
        left = jnp.where(first, 0.0, turn(x[3], 1))
        back = jnp.where(last, x[3], turn(x[4], 127))
        q = [x[0] + x[1], x[1] + x[2], x[2] + x[3]]
        return [
            (left + x[0]) + q[0],
            q[0] + q[1],
            q[1] + q[2],
            q[2] + (x[3] + right),
            (back + x[4]) + (x[4] + turn(x[4], 1)),
        ]

    def apply(part, source, finish):
        def row(i):
            return across([term[source, part, i, v] for v in range(WAYS)])

        known = {i: row(i) for i in (0, OWN - 1, OWN, BLK - 1)}
        down = {i: [pltpu.roll(h, 1, 0) for h in known[i]] for i in (OWN - 1, BLK - 1)}
        up = {i: [pltpu.roll(h, 7, 0) for h in known[i]] for i in (0, OWN)}

        def ends(at, other, same):
            return [jnp.where(sub == at, a, b) for a, b in zip(other, same)]

        def open_ends(at, other, same):
            return [jnp.where(rim[at], 0.0, a) for a in ends(at, other, same)]

        chains = (
            (
                range(OWN),
                known[0],
                open_ends(0, down[BLK - 1], down[OWN - 1]),
                open_ends(7, up[OWN], up[0]),
            ),
            (
                range(OWN, BLK),
                known[OWN],
                ends(0, down[OWN - 1], down[BLK - 1]),
                ends(7, up[0], up[OWN]),
            ),
        )
        for span, h_cur, h_low, h_high in chains:
            pair = [a + b for a, b in zip(h_low, h_cur)]
            for i in span:
                if i == span[-1]:
                    h_next = h_high
                else:
                    h_next = known[i + 1] if i + 1 in known else row(i + 1)
                pair_next = [a + b for a, b in zip(h_cur, h_next)]
                for v in range(WAYS):
                    finish(i, v, pair[v] + pair_next[v])
                pair, h_cur = pair_next, h_next

    def combine(i, v, coef):
        real = imag = None
        for k in range(TOP + 1):
            c_re, c_im = coef(2 * k), coef(2 * k + 1)
            t_re = term[k, 0, i, v]
            t_im = term[k, 1, i, v]
            re = c_re * t_re - c_im * t_im
            im = c_re * t_im + c_im * t_re
            real = re if real is None else real + re
            imag = im if imag is None else imag + im
        term[0, 0, i, v] = real
        term[0, 1, i, v] = imag
        return real

    @pl.loop(0, DEPTHS)
    def _(depth):
        for part in range(2):

            def first_term(i, v, s):
                new = 0.125 * s
                pair_sum[part, i, v] = new
                term[1, part, i, v] = new - term[0, part, i, v]

            apply(part, 0, first_term)

        @pl.loop(1, TOP, unroll=TOP - 1)
        def _(k):
            for part in range(2):

                def next_term(i, v, s):
                    new = 0.25 * s - pair_sum[part, i, v]
                    pair_sum[part, i, v] = new
                    term[k + 1, part, i, v] = new - term[k, part, i, v]

                apply(part, k, next_term)

        def combine_own(ref, step):
            @pl.loop(0, OWN, unroll=16)
            def _(i):
                for v in range(4):
                    img[v, pl.ds(i, 8, stride=PITCH), :] = combine(
                        i, v, lambda n: ref[step, i, v, n]
                    )

        @pl.when(depth < AHEAD)
        def _():
            combine_own(coefs, depth)

        @pl.when(depth >= AHEAD)
        def _():
            combine_own(late_coefs, depth - AHEAD)

        @pl.when(depth < DEPTHS - 1)
        def _():
            for j in range(BLK - OWN):
                for v in range(WAYS):
                    idx = natv[depth, v, pl.ds(j, 8, stride=4), :]
                    combine(OWN + j, v, lambda n: gather_lanes(table[n], idx))
            for i in range(OWN):
                idx = sidev[depth, block(i), :]
                combine(i, 4, lambda n: gather_lanes(table[n], idx))

        slot = jnp.where(depth % 2 == core, 0, 1)
        zl = depth // 2

        @pl.loop(0, 4, unroll=4)
        def _(n):
            t = own_tile(half, n)
            even = (lane // 32) % 2 == 0
            for rg in range(4):
                vals = [img[v, tile_group(t, rg), :] for v in range(4)]
                vals = [a + turn(a, 64) for a in vals]
                a, b = [jnp.where(low, vals[i], vals[i + 2]) for i in range(2)]
                out[slot, (n * 2 + zl) * 2, rows(rg), :] = jnp.where(even, a, turn(b, 32))
                out[slot, (n * 2 + zl) * 2 + 1, rows(rg), :] = jnp.where(even, turn(a, 96), b)


def extrapolate(*operands):
    vmem = pl.BlockSpec(memory_space=pltpu.VMEM)
    return pl.pallas_call(
        kernel,
        out_shape=jax.ShapeDtypeStruct((2, 16, 32, 128), jnp.float32),
        in_specs=[vmem] * 8,
        out_specs=vmem,
        scratch_shapes=[
            pltpu.VMEM((2, WAYS, 32, 128), jnp.float32),
            pltpu.VMEM((DEPTHS, WAYS, 32, 128), jnp.int32),
            pltpu.VMEM((2, 8 * PITCH, 128), jnp.float32),
            pltpu.VMEM((DEPTHS, 8 * PITCH, 128), jnp.int32),
            pltpu.VMEM((TOP + 1, 2, BLK, WAYS, 8, 128), jnp.float32),
            pltpu.VMEM((2, BLK, WAYS, 8, 128), jnp.float32),
            pltpu.VMEM((4, 8 * PITCH, 128), jnp.float32),
        ],
        compiler_params=pltpu.CompilerParams(vmem_limit_bytes=14 * 1024 * 1024),
        cost_estimate=pl.CostEstimate(flops=70_000_000, bytes_accessed=4_000_000, transcendentals=0),
    )(*operands)


def per_device(surface, coef_table, vel_index):
    groups = groups_of_quadrant()

    with jax.named_scope("pack"):
        send = pack(surface, vel_index)
    with jax.named_scope("tables"):
        x, y, zh, zl, core = coordinates()
        xq = jnp.where(x < 2, x, 3 - x)
        yq = jnp.where(y < 2, y, 3 - y)
        freq = core * 32 + (((xq * 2 + zh) * 2 + zl) * 2 + yq) * 2
        own = lax.dynamic_slice(coef_table, (freq, 0, 0, 0), (2, TOP + 1, 2, NV))
    with jax.named_scope("spread"):
        recv = lax.all_to_all(send, AXES, 0, 0, axis_index_groups=groups)
    with jax.named_scope("halo"):
        below, beside, corner, table = edges(recv, own)
        below = lax.ppermute(below, AXES, pairs(lambda x, y, *rest: (3 - x, y, *rest)))
        beside = lax.ppermute(beside, AXES, pairs(lambda x, y, *rest: (x, 3 - y, *rest)))
        corner = lax.ppermute(corner, AXES, pairs(lambda x, y, *rest: (3 - x, 3 - y, *rest)))
    with jax.named_scope("velocity"):
        vel_other = lax.ppermute(recv[:, 2], AXES, core_pairs())
    with jax.named_scope("prepare"):
        start, index, coefs, row_table, zero = prepare(recv, vel_other, table)
    with jax.named_scope("velocity"):
        edge_vel = lax.ppermute(edge_velocity(below, beside, corner, zero), AXES, core_pairs())
    with jax.named_scope("late"):
        late_coefs = late(index, table, row_table)
    with jax.named_scope("extrapolate"):
        out = extrapolate(start, late_coefs, coefs, below, beside, corner, edge_vel, table)
    with jax.named_scope("image"):
        total = out[0] + lax.ppermute(out[1], AXES, core_pairs())
        parts = lax.all_to_all(total, AXES, 0, 0, axis_index_groups=groups)
        return add_up(parts)


def solution(mesh):
    in_specs = (P(None, None, "gx", "gy"), P(), P("sec", "gx", "gy"))
    out_specs = P("sec", "gx", "gy")
    return jax.shard_map(
        per_device, mesh=mesh, in_specs=in_specs, out_specs=out_specs, check_vma=False
    )
```

```python
import jax
import jax.numpy as jnp
from jax import lax
from jax.experimental import pallas as pl
from jax.experimental.pallas import tpu as pltpu
from jax.sharding import PartitionSpec as P

AXES = ("sec", "gx", "gy")
OWN = 16
BLK = 20
PITCH = 24
WAYS = 5
AHEAD = 3
TOP = 8
DEPTHS = 4
NV = 64
COEFS = 2 * (TOP + 1)
HALO_BY_ROW = 4
BY_ROW = 6


def flat(x, y, zh, zl, core):
    return ((zl * 2 + core) * 8 + x * 2 + zh) * 4 + y


def from_rim(half, q):
    return q if half == 0 else 3 - q


def groups_of_quadrant():
    return [
        [
            flat(from_rim(half_x, xq), from_rim(half_y, yq), zh, zl, core)
            for xq in range(2)
            for zh in range(2)
            for zl in range(2)
            for yq in range(2)
        ]
        for half_x in range(2)
        for half_y in range(2)
        for core in range(2)
    ]


def pairs(partner):
    return [
        (flat(x, y, zh, zl, core), flat(*partner(x, y, zh, zl, core)))
        for x in range(4)
        for y in range(4)
        for zh in range(2)
        for zl in range(2)
        for core in range(2)
    ]


def core_pairs():
    return pairs(lambda x, y, zh, zl, core: (x, y, zh, zl, 1 - core))


def gather_lanes(x, idx):
    return jnp.take_along_axis(x, idx, axis=1, mode="promise_in_bounds")


def gather_rows(x, idx):
    return jnp.take_along_axis(x, idx, axis=0, mode="promise_in_bounds")


def look_up(indices, table, row_table, store):
    low = [idx & 7 for idx in indices]
    bits = [[(idx & (8 << b)) == 0 for b in range(3)] for idx in indices]
    for v, idx in enumerate(indices):
        for n in range(BY_ROW, COEFS):
            store(v, n, gather_lanes(table[n], idx))
    for n in range(BY_ROW):
        entries = [row_table[n, j] for j in range(8)]
        for v in range(len(indices)):
            level = [gather_rows(e, low[v]) for e in entries]
            for bit in bits[v]:
                level = [jnp.where(bit, a, b) for a, b in zip(level[::2], level[1::2])]
            store(v, n, level[0])


def lanes():
    return lax.broadcasted_iota(jnp.int32, (8, 128), 1)


def rows(rg):
    return pl.ds(rg * 8, 8)


def turn(x, by):
    return pltpu.roll(x, by, 1)


def swap_blocks(x):
    lane = lanes()
    low = lane < 64
    even = (lane // 32) % 2 == 0
    near = [jnp.where(low, x[i], turn(x[i + 2], 64)) for i in range(2)]
    far = [jnp.where(low, turn(x[i], 64), x[i + 2]) for i in range(2)]
    res = []
    for a, b in (near, far):
        res.append(jnp.where(even, a, turn(b, 32)))
        res.append(jnp.where(even, turn(a, 96), b))
    return res


def coordinates():
    sec, gx, y = lax.axis_index("sec"), lax.axis_index("gx"), lax.axis_index("gy")
    x, zh = gx // 2, gx % 2
    return x, y, zh, sec // 2, sec % 2


def pack_kernel(surface, vel, send, buf, vel_buf, sems):
    _, y, _, zl, core = coordinates()
    lane = lanes()
    idx = 4 * (lane % 32) + lane // 32
    idx = jnp.where(y < 2, idx, 127 - idx)
    vel_copy = pltpu.make_async_copy(vel, vel_buf, sems.at[4])
    vel_copy.start()
    copies = [
        pltpu.make_async_copy(
            surface.at[pl.ds(core * 16 + j * 4, 4), zl], buf.at[pl.ds(j * 4, 4)], sems.at[j]
        )
        for j in range(4)
    ]
    for copy in copies:
        copy.start()
    vel_copy.wait()
    for rg in range(4):
        value = gather_lanes(vel_buf[0, rows(rg), :].astype(jnp.float32), idx)
        for n in range(16):
            send[n, 2, rows(rg), :] = value
    for j, copy in enumerate(copies):
        copy.wait()
        for n in range(j * 4, j * 4 + 4):
            for part in range(2):
                for rg in range(4):
                    send[n, part, rows(rg), :] = gather_lanes(buf[n, part, rows(rg), :], idx)


def pack(surface, vel):
    vmem = pl.BlockSpec(memory_space=pltpu.VMEM)
    return pl.pallas_call(
        pack_kernel,
        out_shape=jax.ShapeDtypeStruct((16, 3, 32, 128), jnp.float32),
        in_specs=[pl.BlockSpec(memory_space=pl.ANY)] * 2,
        out_specs=vmem,
        scratch_shapes=[
            pltpu.VMEM((16, 2, 32, 128), jnp.float32),
            pltpu.VMEM((1, 32, 128), jnp.int32),
            pltpu.SemaphoreType.DMA((5,)),
        ],
        compiler_params=pltpu.CompilerParams(vmem_limit_bytes=60 * 1024 * 1024),
    )(surface.reshape(32, 2, 2, 32, 128), vel)


def sum_kernel(parts, image):
    y = lax.axis_index("gy")
    lane = lanes()
    column = jnp.where(y < 2, lane, 127 - lane)
    idx = 32 * (column % 4) + column // 4
    for rg in range(4):
        terms = [parts[n, rows(rg), :] for n in range(16)]
        while len(terms) > 1:
            terms = [a + b for a, b in zip(terms[::2], terms[1::2])]
        image[0, rows(rg), :] = gather_lanes(terms[0], idx)


def add_up(parts):
    vmem = pl.BlockSpec(memory_space=pltpu.VMEM)
    return pl.pallas_call(
        sum_kernel,
        out_shape=jax.ShapeDtypeStruct((1, 32, 128), jnp.float32),
        in_specs=[vmem],
        out_specs=vmem,
        compiler_params=pltpu.CompilerParams(vmem_limit_bytes=16 * 1024 * 1024),
    )(parts)


def own_tile(half, n):
    return jnp.where(half == 0, n, (n + 2) % 4)


def edge_kernel(recv, own, below, beside, corner, table):
    x, _, _, _, _ = coordinates()
    half = x // 2
    lane = lanes()
    inner = lane % 32
    block = lane // 32
    last = 32 * (inner % 4) + 24 + inner // 4
    edge = 2 + (1 - half)
    for k in range(TOP + 1):
        pair = jnp.concatenate([own[0, k], own[1, k]], axis=1)
        for r in range(2):
            table[2 * k + r] = jnp.broadcast_to(pair[r : r + 1], (8, 128))

    for yq in range(2):
        for rg in range(4):
            for f in range(2):
                for part in range(2):
                    below[(f * 2 + part) * 2 + yq, rows(rg), :] = recv[
                        (edge * 2 + f) * 2 + yq, part, rows(rg), :
                    ]
            if rg < 3:
                zl, row0 = 0, 8 * (1 - half) + rg * 8
            else:
                zl, row0 = 1, 24 * (1 - half)
            below[8 + yq, rows(rg), :] = recv[
                (edge * 2 + zl) * 2 + yq, 2, pl.ds(pl.multiple_of(row0, 8), 8), :
            ]

    def final_columns(n, f, slab, rg):
        return gather_lanes(recv[(n * 2 + f) * 2 + 1, slab, rows(rg), :], last)

    for rg in range(4):
        for slab in range(3):
            a, b = [final_columns(edge, f, slab, rg) for f in range(2)]
            corner[slab, rows(rg), :] = jnp.where(lane < 64, a, b)
            for t in range(2):
                near, far = own_tile(half, t), own_tile(half, t + 2)
                a, b, c, d = [
                    final_columns(n, f, slab, rg) for f in range(2) for n in (far, near)
                ]
                beside[slab, pl.ds(t * 32 + rg * 8, 8), :] = jnp.where(
                    block < 2, jnp.where(block == 0, a, b), jnp.where(block == 2, c, d)
                )


def edges(recv, own):
    vmem = pl.BlockSpec(memory_space=pltpu.VMEM)
    return pl.pallas_call(
        edge_kernel,
        out_shape=(
            jax.ShapeDtypeStruct((10, 32, 128), jnp.float32),
            jax.ShapeDtypeStruct((3, 64, 128), jnp.float32),
            jax.ShapeDtypeStruct((3, 32, 128), jnp.float32),
            jax.ShapeDtypeStruct((COEFS, 8, 128), jnp.float32),
        ),
        in_specs=[vmem] * 2,
        out_specs=(vmem,) * 4,
        compiler_params=pltpu.CompilerParams(vmem_limit_bytes=16 * 1024 * 1024),
    )(recv, own)


def edge_velocity_kernel(below, beside, corner, zero, vel):
    for rg in range(4):
        for q in range(2):
            vel[q, rows(rg), :] = below[8 + q, rows(rg), :] + zero[...]
            vel[2 + q, rows(rg), :] = beside[2, pl.ds(q * 32 + rg * 8, 8), :]
        vel[4, rows(rg), :] = corner[2, rows(rg), :]


def edge_velocity(*operands):
    vmem = pl.BlockSpec(memory_space=pltpu.VMEM)
    return pl.pallas_call(
        edge_velocity_kernel,
        out_shape=jax.ShapeDtypeStruct((5, 32, 128), jnp.float32),
        in_specs=[vmem] * 4,
        out_specs=vmem,
        compiler_params=pltpu.CompilerParams(vmem_limit_bytes=16 * 1024 * 1024),
    )(*operands)


def tile_group(t, rg):
    return pl.ds(pl.multiple_of((2 * t + rg // 2) * PITCH + 8 * (rg % 2), 8), 8)


def prepare_kernel(
    recv, vel_other, table, start, index, coefs, row_table, zero, nat, natv
):
    x, _, _, _, core = coordinates()
    zero[...] = jnp.zeros_like(zero)
    entry = lax.broadcasted_iota(jnp.int32, (8, 128), 0) + jnp.where(lanes() < 64, 0, NV)
    for j in range(8):
        for n in range(BY_ROW):
            row_table[n, j] = gather_lanes(table[n], entry + 8 * j)
    half = x // 2
    shift = jnp.where(lanes() < 64, 0, NV)

    @pl.loop(0, 4)
    def _(n):
        t = own_tile(half, n)
        for rg in range(4):
            dst = tile_group(t, rg)
            for part in range(2):
                vs = swap_blocks([recv[n * 4 + m, part, rows(rg), :] for m in range(4)])
                for v in range(4):
                    nat[part, v, dst, :] = vs[v]
            for zl in range(2):
                for mine in range(2):
                    two = [
                        recv[n * 4 + zl * 2 + yq, 2, rows(rg), :]
                        if mine
                        else vel_other[n * 4 + zl * 2 + yq, rows(rg), :]
                        for yq in range(2)
                    ]
                    depth = zl * 2 + (core if mine else 1 - core)
                    vs = swap_blocks(two + two)
                    for v in range(4):
                        natv[depth, v, dst, :] = vs[v].astype(jnp.int32) + shift

    def block(i):
        return pl.ds(i, 8, stride=PITCH)

    for i in range(OWN):
        for v in range(4):
            for part in range(2):
                start[part, i, v] = nat[part, v, block(i), :]
            for depth in range(AHEAD, DEPTHS):
                index[depth - AHEAD, i, v] = natv[depth, v, block(i), :]

    @pl.loop(0, AHEAD)
    def _(depth):
        @pl.loop(0, OWN, unroll=16)
        def _(i):
            def store(v, n, value):
                coefs[depth, i, v, n] = value

            look_up([natv[depth, v, block(i), :] for v in range(4)], table, row_table, store)


def prepare(recv, vel_other, table):
    vmem = pl.BlockSpec(memory_space=pltpu.VMEM)
    return pl.pallas_call(
        prepare_kernel,
        out_shape=(
            jax.ShapeDtypeStruct((2, OWN, 4, 8, 128), jnp.float32),
            jax.ShapeDtypeStruct((DEPTHS - AHEAD, OWN, 4, 8, 128), jnp.int32),
            jax.ShapeDtypeStruct((AHEAD, OWN, 4, COEFS, 8, 128), jnp.float32),
            jax.ShapeDtypeStruct((BY_ROW, 8, 8, 128), jnp.float32),
            jax.ShapeDtypeStruct((8, 128), jnp.float32),
        ),
        in_specs=[vmem] * 3,
        out_specs=(vmem,) * 5,
        scratch_shapes=[
            pltpu.VMEM((2, 4, 8 * PITCH, 128), jnp.float32),
            pltpu.VMEM((DEPTHS, 4, 8 * PITCH, 128), jnp.int32),
        ],
        compiler_params=pltpu.CompilerParams(vmem_limit_bytes=8 * 1024 * 1024),
        cost_estimate=pl.CostEstimate(flops=20_000_000, bytes_accessed=4_000_000, transcendentals=0),
    )(recv, vel_other, table)


def late_kernel(index, table, row_table, coefs):
    for depth in range(DEPTHS - AHEAD):

        @pl.loop(0, OWN, unroll=16)
        def _(i):
            def store(v, n, value):
                coefs[depth, i, v, n] = value

            look_up([index[depth, i, v] for v in range(4)], table, row_table, store)


def late(index, table, row_table):
    vmem = pl.BlockSpec(memory_space=pltpu.VMEM)
    return pl.pallas_call(
        late_kernel,
        out_shape=jax.ShapeDtypeStruct((DEPTHS - AHEAD, OWN, 4, COEFS, 8, 128), jnp.float32),
        in_specs=[vmem] * 3,
        out_specs=vmem,
        compiler_params=pltpu.CompilerParams(vmem_limit_bytes=8 * 1024 * 1024),
        cost_estimate=pl.CostEstimate(flops=5_000_000, bytes_accessed=1_000_000, transcendentals=0),
    )(index, table, row_table)


def kernel(
    start, late_coefs, coefs, below, beside, corner, vel_other, table, row_table, out,
    nat, natv, side, sidev, term, pair_sum, img
):
    x, _, _, _, core = coordinates()
    half = x // 2
    lane = lanes()
    sub = lax.broadcasted_iota(jnp.int32, (8, 128), 0)
    first = lane % 64 == 0
    last = lane % 64 == 63
    low = lane < 64
    shift = jnp.where(low, 0, NV)
    rim = {0: (sub == 0) & (half == 0), 7: (sub == 7) & (half == 1)}

    def block(i):
        return pl.ds(i, 8, stride=PITCH)

    for part in range(2):
        for rg in range(4):
            vs = swap_blocks(
                [below[(f * 2 + part) * 2 + yq, rows(rg), :] for f in range(2) for yq in range(2)]
            )
            for v in range(4):
                nat[part, v, rows(rg), :] = vs[v]
            nat[part, 4, rows(rg), :] = corner[part, rows(rg), :]

    def both(value, zl):
        other = turn(value, 64)
        return (jnp.where(low, value, other) if zl == 0 else jnp.where(low, other, value)).astype(
            jnp.int32
        ) + shift

    natv[...] = jnp.zeros_like(natv)
    for mine in range(2):
        parity = core if mine else 1 - core
        for rg in range(4):
            two = [below[8 + yq, rows(rg), :] if mine else vel_other[yq, rows(rg), :] for yq in range(2)]
            vs = swap_blocks(two + two)
            if rg < 3:
                row0, depth = jnp.where(half == 0, 0, 8) + rg * 8, parity
            else:
                row0, depth = jnp.where(half == 0, 0, 24), 2 + parity
            for v in range(4):
                natv[depth, v, pl.ds(pl.multiple_of(row0, 8), 8), :] = (
                    vs[v].astype(jnp.int32) + shift
                )
            value = corner[2, rows(rg), :] if mine else vel_other[4, rows(rg), :]
            for zl in range(2):
                natv[2 * zl + parity, 4, rows(rg), :] = both(value, zl)

    for t in range(4):
        for rg in range(4):
            dst = tile_group(t, rg)
            src = pl.ds((t % 2) * 32 + rg * 8, 8)

            def placed(value):
                return value if t < 2 else turn(value, 32)

            for part in range(2):
                side[part, dst, :] = placed(beside[part, src, :])
            for mine in range(2):
                parity = core if mine else 1 - core
                value = placed(beside[2, src, :] if mine else vel_other[2 + t % 2, rows(rg), :])
                for zl in range(2):
                    sidev[2 * zl + parity, dst, :] = both(value, zl)

    for part in range(2):
        for i in range(OWN):
            for v in range(4):
                term[0, part, i, v] = start[part, i, v]
            term[0, part, i, 4] = side[part, block(i), :]
        for j in range(BLK - OWN):
            for v in range(WAYS):
                term[0, part, OWN + j, v] = nat[part, v, pl.ds(j, 8, stride=4), :]

    def across(x):
        right = jnp.where(last, x[4], turn(x[0], 127))
        left = jnp.where(first, 0.0, turn(x[3], 1))
        back = jnp.where(last, x[3], turn(x[4], 127))
        q = [x[0] + x[1], x[1] + x[2], x[2] + x[3]]
        return [
            (left + x[0]) + q[0],
            q[0] + q[1],
            q[1] + q[2],
            q[2] + (x[3] + right),
            (back + x[4]) + (x[4] + turn(x[4], 1)),
        ]

    def apply(part, source, finish):
        def row(i):
            return across([term[source, part, i, v] for v in range(WAYS)])

        known = {i: row(i) for i in (0, OWN - 1, OWN, BLK - 1)}
        down = {i: [pltpu.roll(h, 1, 0) for h in known[i]] for i in (OWN - 1, BLK - 1)}
        up = {i: [pltpu.roll(h, 7, 0) for h in known[i]] for i in (0, OWN)}

        def ends(at, other, same):
            return [jnp.where(sub == at, a, b) for a, b in zip(other, same)]

        def open_ends(at, other, same):
            return [jnp.where(rim[at], 0.0, a) for a in ends(at, other, same)]

        chains = (
            (
                range(OWN),
                known[0],
                open_ends(0, down[BLK - 1], down[OWN - 1]),
                open_ends(7, up[OWN], up[0]),
            ),
            (
                range(OWN, BLK),
                known[OWN],
                ends(0, down[OWN - 1], down[BLK - 1]),
                ends(7, up[0], up[OWN]),
            ),
        )
        for span, h_cur, h_low, h_high in chains:
            pair = [a + b for a, b in zip(h_low, h_cur)]
            for i in span:
                if i == span[-1]:
                    h_next = h_high
                else:
                    h_next = known[i + 1] if i + 1 in known else row(i + 1)
                pair_next = [a + b for a, b in zip(h_cur, h_next)]
                for v in range(WAYS):
                    finish(i, v, pair[v] + pair_next[v])
                pair, h_cur = pair_next, h_next

    def combine(i, v, coef):
        real = imag = None
        for k in range(TOP + 1):
            c_re, c_im = coef(2 * k), coef(2 * k + 1)
            t_re = term[k, 0, i, v]
            t_im = term[k, 1, i, v]
            re = c_re * t_re - c_im * t_im
            im = c_re * t_im + c_im * t_re
            real = re if real is None else real + re
            imag = im if imag is None else imag + im
        term[0, 0, i, v] = real
        term[0, 1, i, v] = imag
        return real

    def halo_coef(idx):
        low = idx & 7
        bits = [(idx & (8 << b)) == 0 for b in range(3)]

        def coef(n):
            if n >= HALO_BY_ROW:
                return gather_lanes(table[n], idx)
            level = [gather_rows(row_table[n, j], low) for j in range(8)]
            for bit in bits:
                level = [jnp.where(bit, a, b) for a, b in zip(level[::2], level[1::2])]
            return level[0]

        return coef

    @pl.loop(0, DEPTHS)
    def _(depth):
        for part in range(2):

            def first_term(i, v, s):
                new = 0.125 * s
                pair_sum[part, i, v] = new
                term[1, part, i, v] = new - term[0, part, i, v]

            apply(part, 0, first_term)

        @pl.loop(1, TOP, unroll=TOP - 1)
        def _(k):
            for part in range(2):

                def next_term(i, v, s):
                    new = 0.25 * s - pair_sum[part, i, v]
                    pair_sum[part, i, v] = new
                    term[k + 1, part, i, v] = new - term[k, part, i, v]

                apply(part, k, next_term)

        def combine_own(ref, step):
            @pl.loop(0, OWN, unroll=16)
            def _(i):
                for v in range(4):
                    img[v, pl.ds(i, 8, stride=PITCH), :] = combine(
                        i, v, lambda n: ref[step, i, v, n]
                    )

        @pl.when(depth < AHEAD)
        def _():
            combine_own(coefs, depth)

        @pl.when(depth >= AHEAD)
        def _():
            combine_own(late_coefs, depth - AHEAD)

        @pl.when(depth < DEPTHS - 1)
        def _():
            for j in range(BLK - OWN):
                for v in range(WAYS):
                    idx = natv[depth, v, pl.ds(j, 8, stride=4), :]
                    combine(OWN + j, v, halo_coef(idx))
            for i in range(OWN):
                idx = sidev[depth, block(i), :]
                combine(i, 4, halo_coef(idx))

        slot = jnp.where(depth % 2 == core, 0, 1)
        zl = depth // 2

        @pl.loop(0, 4, unroll=4)
        def _(n):
            t = own_tile(half, n)
            even = (lane // 32) % 2 == 0
            for rg in range(4):
                vals = [img[v, tile_group(t, rg), :] for v in range(4)]
                vals = [a + turn(a, 64) for a in vals]
                a, b = [jnp.where(low, vals[i], vals[i + 2]) for i in range(2)]
                out[slot, (n * 2 + zl) * 2, rows(rg), :] = jnp.where(even, a, turn(b, 32))
                out[slot, (n * 2 + zl) * 2 + 1, rows(rg), :] = jnp.where(even, turn(a, 96), b)


def extrapolate(*operands):
    vmem = pl.BlockSpec(memory_space=pltpu.VMEM)
    return pl.pallas_call(
        kernel,
        out_shape=jax.ShapeDtypeStruct((2, 16, 32, 128), jnp.float32),
        in_specs=[vmem] * 9,
        out_specs=vmem,
        scratch_shapes=[
            pltpu.VMEM((2, WAYS, 32, 128), jnp.float32),
            pltpu.VMEM((DEPTHS, WAYS, 32, 128), jnp.int32),
            pltpu.VMEM((2, 8 * PITCH, 128), jnp.float32),
            pltpu.VMEM((DEPTHS, 8 * PITCH, 128), jnp.int32),
            pltpu.VMEM((TOP + 1, 2, BLK, WAYS, 8, 128), jnp.float32),
            pltpu.VMEM((2, BLK, WAYS, 8, 128), jnp.float32),
            pltpu.VMEM((4, 8 * PITCH, 128), jnp.float32),
        ],
        compiler_params=pltpu.CompilerParams(vmem_limit_bytes=14 * 1024 * 1024),
        cost_estimate=pl.CostEstimate(flops=70_000_000, bytes_accessed=4_000_000, transcendentals=0),
    )(*operands)


def per_device(surface, coef_table, vel_index):
    groups = groups_of_quadrant()

    with jax.named_scope("pack"):
        send = pack(surface, vel_index)
    with jax.named_scope("tables"):
        x, y, zh, zl, core = coordinates()
        xq = jnp.where(x < 2, x, 3 - x)
        yq = jnp.where(y < 2, y, 3 - y)
        freq = core * 32 + (((xq * 2 + zh) * 2 + zl) * 2 + yq) * 2
        own = lax.dynamic_slice(coef_table, (freq, 0, 0, 0), (2, TOP + 1, 2, NV))
    with jax.named_scope("spread"):
        recv = lax.all_to_all(send, AXES, 0, 0, axis_index_groups=groups)
    with jax.named_scope("halo"):
        below, beside, corner, table = edges(recv, own)
        below = lax.ppermute(below, AXES, pairs(lambda x, y, *rest: (3 - x, y, *rest)))
        beside = lax.ppermute(beside, AXES, pairs(lambda x, y, *rest: (x, 3 - y, *rest)))
        corner = lax.ppermute(corner, AXES, pairs(lambda x, y, *rest: (3 - x, 3 - y, *rest)))
    with jax.named_scope("velocity"):
        vel_other = lax.ppermute(recv[:, 2], AXES, core_pairs())
    with jax.named_scope("prepare"):
        start, index, coefs, row_table, zero = prepare(recv, vel_other, table)
    with jax.named_scope("velocity"):
        edge_vel = lax.ppermute(edge_velocity(below, beside, corner, zero), AXES, core_pairs())
    with jax.named_scope("late"):
        late_coefs = late(index, table, row_table)
    with jax.named_scope("extrapolate"):
        out = extrapolate(
            start, late_coefs, coefs, below, beside, corner, edge_vel, table, row_table
        )
    with jax.named_scope("image"):
        total = out[0] + lax.ppermute(out[1], AXES, core_pairs())
        parts = lax.all_to_all(total, AXES, 0, 0, axis_index_groups=groups)
        return add_up(parts)


def solution(mesh):
    in_specs = (P(None, None, "gx", "gy"), P(), P("sec", "gx", "gy"))
    out_specs = P("sec", "gx", "gy")
    return jax.shard_map(
        per_device, mesh=mesh, in_specs=in_specs, out_specs=out_specs, check_vma=False
    )
```

```python
import jax
import jax.numpy as jnp
from jax import lax
from jax.experimental import pallas as pl
from jax.experimental.pallas import tpu as pltpu
from jax.sharding import PartitionSpec as P

AXES = ("sec", "gx", "gy")
OWN = 16
BLK = 20
PITCH = 24
WAYS = 5
AHEAD = 3
TOP = 8
DEPTHS = 4
NV = 64
COEFS = 2 * (TOP + 1)
HALO_BY_ROW = 6
BY_ROW = 6


def flat(x, y, zh, zl, core):
    return ((zl * 2 + core) * 8 + x * 2 + zh) * 4 + y


def from_rim(half, q):
    return q if half == 0 else 3 - q


def groups_of_quadrant():
    return [
        [
            flat(from_rim(half_x, xq), from_rim(half_y, yq), zh, zl, core)
            for xq in range(2)
            for zh in range(2)
            for zl in range(2)
            for yq in range(2)
        ]
        for half_x in range(2)
        for half_y in range(2)
        for core in range(2)
    ]


def pairs(partner):
    return [
        (flat(x, y, zh, zl, core), flat(*partner(x, y, zh, zl, core)))
        for x in range(4)
        for y in range(4)
        for zh in range(2)
        for zl in range(2)
        for core in range(2)
    ]


def core_pairs():
    return pairs(lambda x, y, zh, zl, core: (x, y, zh, zl, 1 - core))


def gather_lanes(x, idx):
    return jnp.take_along_axis(x, idx, axis=1, mode="promise_in_bounds")


def gather_rows(x, idx):
    return jnp.take_along_axis(x, idx, axis=0, mode="promise_in_bounds")


def look_up(indices, table, row_table, store):
    low = [idx & 7 for idx in indices]
    bits = [[(idx & (8 << b)) == 0 for b in range(3)] for idx in indices]
    for v, idx in enumerate(indices):
        for n in range(BY_ROW, COEFS):
            store(v, n, gather_lanes(table[n], idx))
    for n in range(BY_ROW):
        entries = [row_table[n, j] for j in range(8)]
        for v in range(len(indices)):
            level = [gather_rows(e, low[v]) for e in entries]
            for bit in bits[v]:
                level = [jnp.where(bit, a, b) for a, b in zip(level[::2], level[1::2])]
            store(v, n, level[0])


def lanes():
    return lax.broadcasted_iota(jnp.int32, (8, 128), 1)


def rows(rg):
    return pl.ds(rg * 8, 8)


def turn(x, by):
    return pltpu.roll(x, by, 1)


def swap_blocks(x):
    lane = lanes()
    low = lane < 64
    even = (lane // 32) % 2 == 0
    near = [jnp.where(low, x[i], turn(x[i + 2], 64)) for i in range(2)]
    far = [jnp.where(low, turn(x[i], 64), x[i + 2]) for i in range(2)]
    res = []
    for a, b in (near, far):
        res.append(jnp.where(even, a, turn(b, 32)))
        res.append(jnp.where(even, turn(a, 96), b))
    return res


def coordinates():
    sec, gx, y = lax.axis_index("sec"), lax.axis_index("gx"), lax.axis_index("gy")
    x, zh = gx // 2, gx % 2
    return x, y, zh, sec // 2, sec % 2


def pack_kernel(surface, vel, send, buf, vel_buf, sems):
    _, y, _, zl, core = coordinates()
    lane = lanes()
    idx = 4 * (lane % 32) + lane // 32
    idx = jnp.where(y < 2, idx, 127 - idx)
    vel_copy = pltpu.make_async_copy(vel, vel_buf, sems.at[4])
    vel_copy.start()
    copies = [
        pltpu.make_async_copy(
            surface.at[pl.ds(core * 16 + j * 4, 4), zl], buf.at[pl.ds(j * 4, 4)], sems.at[j]
        )
        for j in range(4)
    ]
    for copy in copies:
        copy.start()
    vel_copy.wait()
    for rg in range(4):
        value = gather_lanes(vel_buf[0, rows(rg), :].astype(jnp.float32), idx)
        for n in range(16):
            send[n, 2, rows(rg), :] = value
    for j, copy in enumerate(copies):
        copy.wait()
        for n in range(j * 4, j * 4 + 4):
            for part in range(2):
                for rg in range(4):
                    send[n, part, rows(rg), :] = gather_lanes(buf[n, part, rows(rg), :], idx)


def pack(surface, vel):
    vmem = pl.BlockSpec(memory_space=pltpu.VMEM)
    return pl.pallas_call(
        pack_kernel,
        out_shape=jax.ShapeDtypeStruct((16, 3, 32, 128), jnp.float32),
        in_specs=[pl.BlockSpec(memory_space=pl.ANY)] * 2,
        out_specs=vmem,
        scratch_shapes=[
            pltpu.VMEM((16, 2, 32, 128), jnp.float32),
            pltpu.VMEM((1, 32, 128), jnp.int32),
            pltpu.SemaphoreType.DMA((5,)),
        ],
        compiler_params=pltpu.CompilerParams(vmem_limit_bytes=60 * 1024 * 1024),
    )(surface.reshape(32, 2, 2, 32, 128), vel)


def sum_kernel(parts, image):
    y = lax.axis_index("gy")
    lane = lanes()
    column = jnp.where(y < 2, lane, 127 - lane)
    idx = 32 * (column % 4) + column // 4
    for rg in range(4):
        terms = [parts[n, rows(rg), :] for n in range(16)]
        while len(terms) > 1:
            terms = [a + b for a, b in zip(terms[::2], terms[1::2])]
        image[0, rows(rg), :] = gather_lanes(terms[0], idx)


def add_up(parts):
    vmem = pl.BlockSpec(memory_space=pltpu.VMEM)
    return pl.pallas_call(
        sum_kernel,
        out_shape=jax.ShapeDtypeStruct((1, 32, 128), jnp.float32),
        in_specs=[vmem],
        out_specs=vmem,
        compiler_params=pltpu.CompilerParams(vmem_limit_bytes=16 * 1024 * 1024),
    )(parts)


def own_tile(half, n):
    return jnp.where(half == 0, n, (n + 2) % 4)


def edge_kernel(recv, own, below, beside, corner, table):
    x, _, _, _, _ = coordinates()
    half = x // 2
    lane = lanes()
    inner = lane % 32
    block = lane // 32
    last = 32 * (inner % 4) + 24 + inner // 4
    edge = 2 + (1 - half)
    for k in range(TOP + 1):
        pair = jnp.concatenate([own[0, k], own[1, k]], axis=1)
        for r in range(2):
            table[2 * k + r] = jnp.broadcast_to(pair[r : r + 1], (8, 128))

    for yq in range(2):
        for rg in range(4):
            for f in range(2):
                for part in range(2):
                    below[(f * 2 + part) * 2 + yq, rows(rg), :] = recv[
                        (edge * 2 + f) * 2 + yq, part, rows(rg), :
                    ]
            if rg < 3:
                zl, row0 = 0, 8 * (1 - half) + rg * 8
            else:
                zl, row0 = 1, 24 * (1 - half)
            below[8 + yq, rows(rg), :] = recv[
                (edge * 2 + zl) * 2 + yq, 2, pl.ds(pl.multiple_of(row0, 8), 8), :
            ]

    def final_columns(n, f, slab, rg):
        return gather_lanes(recv[(n * 2 + f) * 2 + 1, slab, rows(rg), :], last)

    for rg in range(4):
        for slab in range(3):
            a, b = [final_columns(edge, f, slab, rg) for f in range(2)]
            corner[slab, rows(rg), :] = jnp.where(lane < 64, a, b)
            for t in range(2):
                near, far = own_tile(half, t), own_tile(half, t + 2)
                a, b, c, d = [
                    final_columns(n, f, slab, rg) for f in range(2) for n in (far, near)
                ]
                beside[slab, pl.ds(t * 32 + rg * 8, 8), :] = jnp.where(
                    block < 2, jnp.where(block == 0, a, b), jnp.where(block == 2, c, d)
                )


def edges(recv, own):
    vmem = pl.BlockSpec(memory_space=pltpu.VMEM)
    return pl.pallas_call(
        edge_kernel,
        out_shape=(
            jax.ShapeDtypeStruct((10, 32, 128), jnp.float32),
            jax.ShapeDtypeStruct((3, 64, 128), jnp.float32),
            jax.ShapeDtypeStruct((3, 32, 128), jnp.float32),
            jax.ShapeDtypeStruct((COEFS, 8, 128), jnp.float32),
        ),
        in_specs=[vmem] * 2,
        out_specs=(vmem,) * 4,
        compiler_params=pltpu.CompilerParams(vmem_limit_bytes=16 * 1024 * 1024),
    )(recv, own)


def edge_velocity_kernel(below, beside, corner, zero, vel):
    for rg in range(4):
        for q in range(2):
            vel[q, rows(rg), :] = below[8 + q, rows(rg), :] + zero[...]
            vel[2 + q, rows(rg), :] = beside[2, pl.ds(q * 32 + rg * 8, 8), :]
        vel[4, rows(rg), :] = corner[2, rows(rg), :]


def edge_velocity(*operands):
    vmem = pl.BlockSpec(memory_space=pltpu.VMEM)
    return pl.pallas_call(
        edge_velocity_kernel,
        out_shape=jax.ShapeDtypeStruct((5, 32, 128), jnp.float32),
        in_specs=[vmem] * 4,
        out_specs=vmem,
        compiler_params=pltpu.CompilerParams(vmem_limit_bytes=16 * 1024 * 1024),
    )(*operands)


def tile_group(t, rg):
    return pl.ds(pl.multiple_of((2 * t + rg // 2) * PITCH + 8 * (rg % 2), 8), 8)


def prepare_kernel(
    recv, vel_other, table, start, index, coefs, row_table, zero, nat, natv
):
    x, _, _, _, core = coordinates()
    zero[...] = jnp.zeros_like(zero)
    entry = lax.broadcasted_iota(jnp.int32, (8, 128), 0) + jnp.where(lanes() < 64, 0, NV)
    for j in range(8):
        for n in range(BY_ROW):
            row_table[n, j] = gather_lanes(table[n], entry + 8 * j)
    half = x // 2
    shift = jnp.where(lanes() < 64, 0, NV)

    @pl.loop(0, 4)
    def _(n):
        t = own_tile(half, n)
        for rg in range(4):
            dst = tile_group(t, rg)
            for part in range(2):
                vs = swap_blocks([recv[n * 4 + m, part, rows(rg), :] for m in range(4)])
                for v in range(4):
                    nat[part, v, dst, :] = vs[v]
            for zl in range(2):
                for mine in range(2):
                    two = [
                        recv[n * 4 + zl * 2 + yq, 2, rows(rg), :]
                        if mine
                        else vel_other[n * 4 + zl * 2 + yq, rows(rg), :]
                        for yq in range(2)
                    ]
                    depth = zl * 2 + (core if mine else 1 - core)
                    vs = swap_blocks(two + two)
                    for v in range(4):
                        natv[depth, v, dst, :] = vs[v].astype(jnp.int32) + shift

    def block(i):
        return pl.ds(i, 8, stride=PITCH)

    for i in range(OWN):
        for v in range(4):
            for part in range(2):
                start[part, i, v] = nat[part, v, block(i), :]
            for depth in range(AHEAD, DEPTHS):
                index[depth - AHEAD, i, v] = natv[depth, v, block(i), :]

    @pl.loop(0, AHEAD)
    def _(depth):
        @pl.loop(0, OWN, unroll=16)
        def _(i):
            def store(v, n, value):
                coefs[depth, i, v, n] = value

            look_up([natv[depth, v, block(i), :] for v in range(4)], table, row_table, store)


def prepare(recv, vel_other, table):
    vmem = pl.BlockSpec(memory_space=pltpu.VMEM)
    return pl.pallas_call(
        prepare_kernel,
        out_shape=(
            jax.ShapeDtypeStruct((2, OWN, 4, 8, 128), jnp.float32),
            jax.ShapeDtypeStruct((DEPTHS - AHEAD, OWN, 4, 8, 128), jnp.int32),
            jax.ShapeDtypeStruct((AHEAD, OWN, 4, COEFS, 8, 128), jnp.float32),
            jax.ShapeDtypeStruct((BY_ROW, 8, 8, 128), jnp.float32),
            jax.ShapeDtypeStruct((8, 128), jnp.float32),
        ),
        in_specs=[vmem] * 3,
        out_specs=(vmem,) * 5,
        scratch_shapes=[
            pltpu.VMEM((2, 4, 8 * PITCH, 128), jnp.float32),
            pltpu.VMEM((DEPTHS, 4, 8 * PITCH, 128), jnp.int32),
        ],
        compiler_params=pltpu.CompilerParams(vmem_limit_bytes=8 * 1024 * 1024),
        cost_estimate=pl.CostEstimate(flops=20_000_000, bytes_accessed=4_000_000, transcendentals=0),
    )(recv, vel_other, table)


def late_kernel(index, table, row_table, coefs):
    for depth in range(DEPTHS - AHEAD):

        @pl.loop(0, OWN, unroll=16)
        def _(i):
            def store(v, n, value):
                coefs[depth, i, v, n] = value

            look_up([index[depth, i, v] for v in range(4)], table, row_table, store)


def late(index, table, row_table):
    vmem = pl.BlockSpec(memory_space=pltpu.VMEM)
    return pl.pallas_call(
        late_kernel,
        out_shape=jax.ShapeDtypeStruct((DEPTHS - AHEAD, OWN, 4, COEFS, 8, 128), jnp.float32),
        in_specs=[vmem] * 3,
        out_specs=vmem,
        compiler_params=pltpu.CompilerParams(vmem_limit_bytes=8 * 1024 * 1024),
        cost_estimate=pl.CostEstimate(flops=5_000_000, bytes_accessed=1_000_000, transcendentals=0),
    )(index, table, row_table)


def kernel(
    start, late_coefs, coefs, below, beside, corner, vel_other, table, row_table, out,
    nat, natv, side, sidev, term, pair_sum, img
):
    x, _, _, _, core = coordinates()
    half = x // 2
    lane = lanes()
    sub = lax.broadcasted_iota(jnp.int32, (8, 128), 0)
    first = lane % 64 == 0
    last = lane % 64 == 63
    low = lane < 64
    shift = jnp.where(low, 0, NV)
    rim = {0: (sub == 0) & (half == 0), 7: (sub == 7) & (half == 1)}

    def block(i):
        return pl.ds(i, 8, stride=PITCH)

    for part in range(2):
        for rg in range(4):
            vs = swap_blocks(
                [below[(f * 2 + part) * 2 + yq, rows(rg), :] for f in range(2) for yq in range(2)]
            )
            for v in range(4):
                nat[part, v, rows(rg), :] = vs[v]
            nat[part, 4, rows(rg), :] = corner[part, rows(rg), :]

    def both(value, zl):
        other = turn(value, 64)
        return (jnp.where(low, value, other) if zl == 0 else jnp.where(low, other, value)).astype(
            jnp.int32
        ) + shift

    natv[...] = jnp.zeros_like(natv)
    for mine in range(2):
        parity = core if mine else 1 - core
        for rg in range(4):
            two = [below[8 + yq, rows(rg), :] if mine else vel_other[yq, rows(rg), :] for yq in range(2)]
            vs = swap_blocks(two + two)
            if rg < 3:
                row0, depth = jnp.where(half == 0, 0, 8) + rg * 8, parity
            else:
                row0, depth = jnp.where(half == 0, 0, 24), 2 + parity
            for v in range(4):
                natv[depth, v, pl.ds(pl.multiple_of(row0, 8), 8), :] = (
                    vs[v].astype(jnp.int32) + shift
                )
            value = corner[2, rows(rg), :] if mine else vel_other[4, rows(rg), :]
            for zl in range(2):
                natv[2 * zl + parity, 4, rows(rg), :] = both(value, zl)

    for t in range(4):
        for rg in range(4):
            dst = tile_group(t, rg)
            src = pl.ds((t % 2) * 32 + rg * 8, 8)

            def placed(value):
                return value if t < 2 else turn(value, 32)

            for part in range(2):
                side[part, dst, :] = placed(beside[part, src, :])
            for mine in range(2):
                parity = core if mine else 1 - core
                value = placed(beside[2, src, :] if mine else vel_other[2 + t % 2, rows(rg), :])
                for zl in range(2):
                    sidev[2 * zl + parity, dst, :] = both(value, zl)

    for part in range(2):
        for i in range(OWN):
            for v in range(4):
                term[0, part, i, v] = start[part, i, v]
            term[0, part, i, 4] = side[part, block(i), :]
        for j in range(BLK - OWN):
            for v in range(WAYS):
                term[0, part, OWN + j, v] = nat[part, v, pl.ds(j, 8, stride=4), :]

    def across(x):
        right = jnp.where(last, x[4], turn(x[0], 127))
        left = jnp.where(first, 0.0, turn(x[3], 1))
        back = jnp.where(last, x[3], turn(x[4], 127))
        q = [x[0] + x[1], x[1] + x[2], x[2] + x[3]]
        return [
            (left + x[0]) + q[0],
            q[0] + q[1],
            q[1] + q[2],
            q[2] + (x[3] + right),
            (back + x[4]) + (x[4] + turn(x[4], 1)),
        ]

    def apply(part, source, finish):
        def row(i):
            return across([term[source, part, i, v] for v in range(WAYS)])

        known = {i: row(i) for i in (0, OWN - 1, OWN, BLK - 1)}
        down = {i: [pltpu.roll(h, 1, 0) for h in known[i]] for i in (OWN - 1, BLK - 1)}
        up = {i: [pltpu.roll(h, 7, 0) for h in known[i]] for i in (0, OWN)}

        def ends(at, other, same):
            return [jnp.where(sub == at, a, b) for a, b in zip(other, same)]

        def open_ends(at, other, same):
            return [jnp.where(rim[at], 0.0, a) for a in ends(at, other, same)]

        chains = (
            (
                range(OWN),
                known[0],
                open_ends(0, down[BLK - 1], down[OWN - 1]),
                open_ends(7, up[OWN], up[0]),
            ),
            (
                range(OWN, BLK),
                known[OWN],
                ends(0, down[OWN - 1], down[BLK - 1]),
                ends(7, up[0], up[OWN]),
            ),
        )
        for span, h_cur, h_low, h_high in chains:
            pair = [a + b for a, b in zip(h_low, h_cur)]
            for i in span:
                if i == span[-1]:
                    h_next = h_high
                else:
                    h_next = known[i + 1] if i + 1 in known else row(i + 1)
                pair_next = [a + b for a, b in zip(h_cur, h_next)]
                for v in range(WAYS):
                    finish(i, v, pair[v] + pair_next[v])
                pair, h_cur = pair_next, h_next

    def combine(i, v, coef):
        real = imag = None
        for k in range(TOP + 1):
            c_re, c_im = coef(2 * k), coef(2 * k + 1)
            t_re = term[k, 0, i, v]
            t_im = term[k, 1, i, v]
            re = c_re * t_re - c_im * t_im
            im = c_re * t_im + c_im * t_re
            real = re if real is None else real + re
            imag = im if imag is None else imag + im
        term[0, 0, i, v] = real
        term[0, 1, i, v] = imag
        return real

    def halo_coef(idx):
        low = idx & 7
        bits = [(idx & (8 << b)) == 0 for b in range(3)]

        def coef(n):
            if n >= HALO_BY_ROW:
                return gather_lanes(table[n], idx)
            level = [gather_rows(row_table[n, j], low) for j in range(8)]
            for bit in bits:
                level = [jnp.where(bit, a, b) for a, b in zip(level[::2], level[1::2])]
            return level[0]

        return coef

    @pl.loop(0, DEPTHS)
    def _(depth):
        for part in range(2):

            def first_term(i, v, s):
                new = 0.125 * s
                pair_sum[part, i, v] = new
                term[1, part, i, v] = new - term[0, part, i, v]

            apply(part, 0, first_term)

        @pl.loop(1, TOP, unroll=TOP - 1)
        def _(k):
            for part in range(2):

                def next_term(i, v, s):
                    new = 0.25 * s - pair_sum[part, i, v]
                    pair_sum[part, i, v] = new
                    term[k + 1, part, i, v] = new - term[k, part, i, v]

                apply(part, k, next_term)

        def combine_own(ref, step):
            @pl.loop(0, OWN, unroll=16)
            def _(i):
                for v in range(4):
                    img[v, pl.ds(i, 8, stride=PITCH), :] = combine(
                        i, v, lambda n: ref[step, i, v, n]
                    )

        @pl.when(depth < AHEAD)
        def _():
            combine_own(coefs, depth)

        @pl.when(depth >= AHEAD)
        def _():
            combine_own(late_coefs, depth - AHEAD)

        @pl.when(depth < DEPTHS - 1)
        def _():
            for j in range(BLK - OWN):
                for v in range(WAYS):
                    idx = natv[depth, v, pl.ds(j, 8, stride=4), :]
                    combine(OWN + j, v, halo_coef(idx))
            for i in range(OWN):
                idx = sidev[depth, block(i), :]
                combine(i, 4, halo_coef(idx))

        slot = jnp.where(depth % 2 == core, 0, 1)
        zl = depth // 2

        @pl.loop(0, 4, unroll=4)
        def _(n):
            t = own_tile(half, n)
            even = (lane // 32) % 2 == 0
            for rg in range(4):
                vals = [img[v, tile_group(t, rg), :] for v in range(4)]
                vals = [a + turn(a, 64) for a in vals]
                a, b = [jnp.where(low, vals[i], vals[i + 2]) for i in range(2)]
                out[slot, (n * 2 + zl) * 2, rows(rg), :] = jnp.where(even, a, turn(b, 32))
                out[slot, (n * 2 + zl) * 2 + 1, rows(rg), :] = jnp.where(even, turn(a, 96), b)


def extrapolate(*operands):
    vmem = pl.BlockSpec(memory_space=pltpu.VMEM)
    return pl.pallas_call(
        kernel,
        out_shape=jax.ShapeDtypeStruct((2, 16, 32, 128), jnp.float32),
        in_specs=[vmem] * 9,
        out_specs=vmem,
        scratch_shapes=[
            pltpu.VMEM((2, WAYS, 32, 128), jnp.float32),
            pltpu.VMEM((DEPTHS, WAYS, 32, 128), jnp.int32),
            pltpu.VMEM((2, 8 * PITCH, 128), jnp.float32),
            pltpu.VMEM((DEPTHS, 8 * PITCH, 128), jnp.int32),
            pltpu.VMEM((TOP + 1, 2, BLK, WAYS, 8, 128), jnp.float32),
            pltpu.VMEM((2, BLK, WAYS, 8, 128), jnp.float32),
            pltpu.VMEM((4, 8 * PITCH, 128), jnp.float32),
        ],
        compiler_params=pltpu.CompilerParams(vmem_limit_bytes=14 * 1024 * 1024),
        cost_estimate=pl.CostEstimate(flops=70_000_000, bytes_accessed=4_000_000, transcendentals=0),
    )(*operands)


def per_device(surface, coef_table, vel_index):
    groups = groups_of_quadrant()

    with jax.named_scope("pack"):
        send = pack(surface, vel_index)
    with jax.named_scope("tables"):
        x, y, zh, zl, core = coordinates()
        xq = jnp.where(x < 2, x, 3 - x)
        yq = jnp.where(y < 2, y, 3 - y)
        freq = core * 32 + (((xq * 2 + zh) * 2 + zl) * 2 + yq) * 2
        own = lax.dynamic_slice(coef_table, (freq, 0, 0, 0), (2, TOP + 1, 2, NV))
    with jax.named_scope("spread"):
        recv = lax.all_to_all(send, AXES, 0, 0, axis_index_groups=groups)
    with jax.named_scope("halo"):
        below, beside, corner, table = edges(recv, own)
        below = lax.ppermute(below, AXES, pairs(lambda x, y, *rest: (3 - x, y, *rest)))
        beside = lax.ppermute(beside, AXES, pairs(lambda x, y, *rest: (x, 3 - y, *rest)))
        corner = lax.ppermute(corner, AXES, pairs(lambda x, y, *rest: (3 - x, 3 - y, *rest)))
    with jax.named_scope("velocity"):
        vel_other = lax.ppermute(recv[:, 2], AXES, core_pairs())
    with jax.named_scope("prepare"):
        start, index, coefs, row_table, zero = prepare(recv, vel_other, table)
    with jax.named_scope("velocity"):
        edge_vel = lax.ppermute(edge_velocity(below, beside, corner, zero), AXES, core_pairs())
    with jax.named_scope("late"):
        late_coefs = late(index, table, row_table)
    with jax.named_scope("extrapolate"):
        out = extrapolate(
            start, late_coefs, coefs, below, beside, corner, edge_vel, table, row_table
        )
    with jax.named_scope("image"):
        total = out[0] + lax.ppermute(out[1], AXES, core_pairs())
        parts = lax.all_to_all(total, AXES, 0, 0, axis_index_groups=groups)
        return add_up(parts)


def solution(mesh):
    in_specs = (P(None, None, "gx", "gy"), P(), P("sec", "gx", "gy"))
    out_specs = P("sec", "gx", "gy")
    return jax.shard_map(
        per_device, mesh=mesh, in_specs=in_specs, out_specs=out_specs, check_vma=False
    )
```
